256 devices in a mesh: dp: 8 (over y, core), ctx: 32 (over x, z).
Axes of the slice: x: 4, y: 4, z: 8, core: 2. Of those that a mesh axis runs over, the one named last changes fastest.
Arguments:
- query_matrix_rows: bfloat16 [8, 4096, 8192], P('dp', 'ctx'), may hold values from -768 to 768
- key_matrix_rows: bfloat16 [8, 4096, 512], P('dp', 'ctx'), may hold values from -7 to 7
- value_matrix_rows: bfloat16 [8, 4096, 512], P('dp', 'ctx'), may hold values from -6 to 6
- adapter_output_gradient: bfloat16 [8, 4096, 16384], P('dp', 'ctx'), may hold values from -0.3984375 to 0.3984375
- head_output_gradient: bfloat16 [8, 4096, 8192], P('dp', 'ctx'), may hold values from -0.3984375 to 0.3984375
- sink_score_bias: float32 [64], P('ctx'), may hold values from 1 to 4
- windows: int32 [8], P('dp'), may hold values from 256 to 1024, as said below
- sink_token_count: int32 [8], P('dp'), may hold values from 1 to 16, as said below
- adapter_down_weight: bfloat16 [128, 8192], P(None, 'ctx'), may hold values from -0.0625 to 0.0625
- adapter_up_weight: bfloat16 [16384, 128], P('ctx'), may hold values from -0.5 to 0.5
Outputs:
- grad_down: float32 [128, 8192], P(None, 'ctx')
- grad_up: float32 [16384, 128], P('ctx')
- grad_bias: float32 [64], P('ctx')
The draws below stay inside these ranges and needn't reach their ends.
Inputs may be any that keep to these rules, and one draw needn't show every extreme that they name: `windows`: some sequence has the window 1024. `sink_token_count`: some sequence has 16 sink tokens.
All inputs are finite; a program needn't handle non-finite values.
Results may differ from the reference program's by a relative error of at most 0.02.
Values may be sent and summed in bfloat16 or wider, within the bound.
A program may use at most 128 MiB of HBM per device.

```python
import jax
import jax.numpy as jnp
from jax import lax

MODEL_DIM = 16384
HEAD_DIM = 128
QUERY_HEADCOUNT = 64
KEY_VALUE_HEADS = 4
LOW_RANK = 128
WIN = 1024
SINK_MAX = 16
SEQUENCE_TOKENS = 4096
N_DP = 8


def shared_pairs(key):
    unbiased_scores = jnp.clip(jax.random.normal(key, (N_DP, SEQUENCE_TOKENS, KEY_VALUE_HEADS, HEAD_DIM), jnp.float32), -6.0, 6.0)
    return unbiased_scores


def draw_key_matrix_rows(key, part):
    unbiased_scores = shared_pairs(key)
    return unbiased_scores.reshape(N_DP, SEQUENCE_TOKENS, KEY_VALUE_HEADS * HEAD_DIM).astype(jnp.bfloat16)


def draw_query_matrix_rows(key, part):
    key = jax.random.fold_in(key, 5)
    queries = jnp.clip(jax.random.normal(key, (N_DP, SEQUENCE_TOKENS, QUERY_HEADCOUNT, HEAD_DIM), jnp.float32), -6.0, 6.0)
    return queries.reshape(N_DP, SEQUENCE_TOKENS, QUERY_HEADCOUNT * HEAD_DIM).astype(jnp.bfloat16)


def draw_windows(key, part):
    key = jax.random.fold_in(key, 7)
    drawn = jax.random.randint(key, (N_DP,), WIN // 4, WIN + 1)
    picked = jax.random.randint(jax.random.fold_in(key, 1), (), 0, N_DP)
    return jnp.where(jnp.arange(N_DP) == picked, WIN, drawn).astype(jnp.int32)


def draw_sink_token_count(key, part):
    key = jax.random.fold_in(key, 9)
    drawn = jax.random.randint(key, (N_DP,), 1, SINK_MAX + 1)
    picked = jax.random.randint(jax.random.fold_in(key, 1), (), 0, N_DP)
    return jnp.where(jnp.arange(N_DP) == picked, SINK_MAX, drawn).astype(jnp.int32)


def raised(result, rng, source, target, parts, factor):
    owner, partner = [(jnp.arange(result.shape[axis_at]) // (result.shape[axis_at] // parts)).reshape([-1 if axis == axis_at else 1 for axis in range(result.ndim)]) for axis_at in (source, target)]
    chosen = jax.random.permutation(rng, parts)[partner]
    strong = (owner == chosen) | (owner == (partner + parts // 2) % parts)
    return jnp.where(strong, factor * result, result)


def levels(own_key, shape, split, low, high):
    def one(axis_at, shards_of):
        steps = jax.random.uniform(jax.random.fold_in(jax.random.fold_in(own_key, 6), axis_at), (shards_of,), jnp.float32, low / len(split), high / len(split))
        return jnp.repeat(jnp.exp(steps), shape[axis_at] // shards_of).reshape((-1,) + (1,) * (len(shape) - axis_at - 1))

    loudness = one(*split[0])
    for cut in split[1:]:
        loudness = loudness * one(*cut)
    return loudness


def normal_values(own_key, shape, scale, limit, shards=(), kind=jnp.bfloat16):
    values = jax.random.normal(own_key, shape, jnp.float32) * scale
    if len(shards) > 0:
        values = levels(own_key, shape, shards, -0.22, 0.18) * values
    return jnp.clip(values, min=-limit, max=limit).astype(kind)


def heavy_noise(key, dims, scale, limit, split, heavy, kind=jnp.bfloat16):
    entries = scale * jax.random.normal(key, dims, jnp.float32)
    if split:
        entries = entries * levels(key, dims, split, -0.22, 0.18)
    return jnp.clip(raised(entries, jax.random.fold_in(key, 3), *heavy), -limit, limit).astype(kind)


def setup_inputs(seed: int = 0) -> dict:
    key_list = jax.random.split(jax.random.key(seed), 11)
    query_matrix_rows = draw_query_matrix_rows(jax.random.fold_in(key_list[10], 71), 0)
    key_matrix_rows = draw_key_matrix_rows(jax.random.fold_in(key_list[10], 71), 0)
    value_matrix_rows = normal_values(key_list[2], (N_DP, SEQUENCE_TOKENS, KEY_VALUE_HEADS * HEAD_DIM), 1.0, 6.0, ((0, 8), (1, 32)))
    adapter_output_gradient = heavy_noise(key_list[3], (N_DP, SEQUENCE_TOKENS, MODEL_DIM), 0.05, 0.3984375, ((0, 8), (1, 32)), (1, 2, 32, 2.75))
    head_output_gradient = normal_values(key_list[4], (N_DP, SEQUENCE_TOKENS, QUERY_HEADCOUNT * HEAD_DIM), 0.05, 0.3984375, ((0, 8), (1, 32)))
    sink_score_bias = jnp.clip(1.0 + 3.0 * jax.random.uniform(key_list[5], (QUERY_HEADCOUNT,), jnp.float32) ** levels(key_list[5], (QUERY_HEADCOUNT,), ((0, 32),), -0.2, 0.2), 1.0, 4.0)
    windows = draw_windows(jax.random.fold_in(key_list[10], 71), 0)
    sink_token_count = draw_sink_token_count(jax.random.fold_in(key_list[10], 71), 0)
    adapter_down_weight = normal_values(key_list[8], (LOW_RANK, QUERY_HEADCOUNT * HEAD_DIM), (QUERY_HEADCOUNT * HEAD_DIM) ** -0.5, 0.0625, ((1, 32),))
    adapter_up_weight = normal_values(key_list[9], (MODEL_DIM, LOW_RANK), LOW_RANK ** -0.5, 0.5, ((0, 32),))
    return {"query_matrix_rows": query_matrix_rows, "key_matrix_rows": key_matrix_rows, "value_matrix_rows": value_matrix_rows, "adapter_output_gradient": adapter_output_gradient, "head_output_gradient": head_output_gradient, "sink_score_bias": sink_score_bias, "windows": windows, "sink_token_count": sink_token_count, "adapter_down_weight": adapter_down_weight, "adapter_up_weight": adapter_up_weight}


adapter_scale_factor = 2.0
masked = -1e30


def attend_sequence(query_seq, key_seq, value_seq, grad_seq, sink_score_bias, window_size, sink_count):
    block_rows = min(512, SEQUENCE_TOKENS)
    span = min(WIN + block_rows, SEQUENCE_TOKENS)
    score_scale = HEAD_DIM ** -0.5
    bias_gradient_table = sink_score_bias.reshape(KEY_VALUE_HEADS, QUERY_HEADCOUNT // KEY_VALUE_HEADS)
    sink_keys = key_seq[:SINK_MAX].astype(jnp.float32)
    sink_values = value_seq[:SINK_MAX].astype(jnp.float32)

    def one_block(block_index):
        query_start = block_index * block_rows
        key_start = jnp.clip(query_start + block_rows - span, 0, SEQUENCE_TOKENS - span).astype(jnp.int32)
        query_block = lax.dynamic_slice_in_dim(query_seq, query_start, block_rows, 0).astype(jnp.float32)
        grad_block = lax.dynamic_slice_in_dim(grad_seq, query_start, block_rows, 0).astype(jnp.float32)
        local_keys = lax.dynamic_slice_in_dim(key_seq, key_start, span, 0).astype(jnp.float32)
        local_values = lax.dynamic_slice_in_dim(value_seq, key_start, span, 0).astype(jnp.float32)
        row_ids = query_start + jnp.arange(block_rows, dtype=jnp.int32)
        col_ids = key_start + jnp.arange(span, dtype=jnp.int32)
        sink_ids = jnp.arange(SINK_MAX, dtype=jnp.int32)
        local_ok = (col_ids[None, :] <= row_ids[:, None]) & (row_ids[:, None] - col_ids[None, :] < window_size) & (col_ids[None, :] >= sink_count)
        sink_ok = (sink_ids[None, :] <= row_ids[:, None]) & (sink_ids[None, :] < sink_count)
        local_score = jnp.einsum("qhgd,khd->hgqk", query_block, local_keys) * score_scale
        sink_score = jnp.einsum("qhgd,khd->hgqk", query_block, sink_keys) * score_scale + bias_gradient_table[:, :, None, None]
        local_score = jnp.where(local_ok, local_score, masked)
        sink_score = jnp.where(sink_ok, sink_score, masked)
        row_max = jnp.maximum(local_score.max(-1), sink_score.max(-1))
        local_exp = jnp.exp(local_score - row_max[..., None])
        sink_exp = jnp.exp(sink_score - row_max[..., None])
        row_total = local_exp.sum(-1) + sink_exp.sum(-1)
        local_prob = local_exp / row_total[..., None]
        sink_prob = sink_exp / row_total[..., None]
        local_weight = lax.optimization_barrier(local_prob.astype(jnp.bfloat16)).astype(jnp.float32)
        sink_weight = lax.optimization_barrier(sink_prob.astype(jnp.bfloat16)).astype(jnp.float32)
        attention_head_output = (jnp.einsum("hgqk,khd->qhgd", local_weight, local_values) + jnp.einsum("hgqk,khd->qhgd", sink_weight, sink_values)).astype(jnp.bfloat16)
        dot_sum = jnp.einsum("qhgd,qhgd->hgq", grad_block, attention_head_output.astype(jnp.float32))
        sink_dot = jnp.einsum("qhgd,khd->hgqk", grad_block, sink_values)
        bias_part = jnp.sum(sink_prob * (sink_dot - dot_sum[..., None]), axis=(2, 3))
        return attention_head_output, bias_part

    head_outs, bias_parts = lax.map(one_block, jnp.arange(SEQUENCE_TOKENS // block_rows, dtype=jnp.int32))
    return head_outs.reshape(SEQUENCE_TOKENS, QUERY_HEADCOUNT * HEAD_DIM), bias_parts.sum(0).reshape(QUERY_HEADCOUNT)


def reference(query_matrix_rows, key_matrix_rows, value_matrix_rows, adapter_output_gradient, head_output_gradient, sink_score_bias, windows, sink_token_count, adapter_down_weight, adapter_up_weight):
    query_group_width = QUERY_HEADCOUNT // KEY_VALUE_HEADS

    def one_sequence(carry, inputs):
        single_sequence_queries, single_sequence_keys, single_sequence_values, single_adapter_gradient, single_head_output, window_size, sink_count = inputs
        rank_space_gradient = jnp.dot(single_adapter_gradient, adapter_up_weight, preferred_element_type=jnp.float32).astype(jnp.bfloat16)
        head_output_total = (single_head_output.astype(jnp.float32) + adapter_scale_factor * jnp.dot(rank_space_gradient, adapter_down_weight, preferred_element_type=jnp.float32)).astype(jnp.bfloat16)
        attention_head_output, sink_bias_gradient = attend_sequence(
            single_sequence_queries.reshape(SEQUENCE_TOKENS, KEY_VALUE_HEADS, query_group_width, HEAD_DIM),
            single_sequence_keys.reshape(SEQUENCE_TOKENS, KEY_VALUE_HEADS, HEAD_DIM),
            single_sequence_values.reshape(SEQUENCE_TOKENS, KEY_VALUE_HEADS, HEAD_DIM),
            head_output_total.reshape(SEQUENCE_TOKENS, KEY_VALUE_HEADS, query_group_width, HEAD_DIM),
            sink_score_bias, window_size, sink_count)
        rank_space_output = jnp.dot(attention_head_output, adapter_down_weight.T, preferred_element_type=jnp.float32).astype(jnp.bfloat16)
        up_gradient_piece = jnp.dot(single_adapter_gradient.T, rank_space_output, preferred_element_type=jnp.float32)
        down_gradient_piece = jnp.dot(rank_space_gradient.T, attention_head_output, preferred_element_type=jnp.float32)
        up_gradient_total, down_gradient_total, bias_gradient_total = carry
        return (up_gradient_total + adapter_scale_factor * up_gradient_piece, down_gradient_total + adapter_scale_factor * down_gradient_piece, bias_gradient_total + sink_bias_gradient), None

    start_sums = (jnp.zeros((MODEL_DIM, LOW_RANK), jnp.float32), jnp.zeros((LOW_RANK, QUERY_HEADCOUNT * HEAD_DIM), jnp.float32), jnp.zeros((QUERY_HEADCOUNT,), jnp.float32))
    sums, unused = lax.scan(one_sequence, start_sums, (query_matrix_rows, key_matrix_rows, value_matrix_rows, adapter_output_gradient, head_output_gradient, windows, sink_token_count))
    up_gradient_total, down_gradient_total, bias_gradient_total = sums
    return down_gradient_total, up_gradient_total, bias_gradient_total
```

```python
import jax
import jax.numpy as jnp
from jax import lax
from jax.experimental import pallas as pl
from jax.experimental.pallas import tpu as pltpu
from jax.sharding import PartitionSpec as P

NX, NY, NZ = 4, 4, 8
N_CTX, N_DP = NX * NZ, NY * 2
TOK = 128
HEAD_DIM = 128
KV_HEADS = 4
GROUP = 16
HEADS = KV_HEADS * GROUP
RANK = 128
SINKS = 16
BLOCKS = 9
UP_ROWS, DOWN_ROWS = 32, 16
CHUNK = UP_ROWS + DOWN_ROWS
HEAD_STEP = 4
MASKED = -1e30
LOG2E = 1.4426950408889634
SCORE_SCALE = LOG2E * HEAD_DIM**-0.5
BF16, F32 = jnp.bfloat16, jnp.float32
MESH = pl.DeviceIdType.MESH

ORDER = (1, 2, 3, 4, 5, 6, 7, 0, 8)
MAIN = 7 * TOK
COLS = 10 * TOK


def dot(a, b):
    return lax.dot_general(a, b, (((1,), (0,)), ((), ())), preferred_element_type=F32)


def dot_nt(a, b):
    return lax.dot_general(a, b, (((1,), (1,)), ((), ())), preferred_element_type=F32)


def kernel(
    bias_ref, win_ref, cnt_ref, q_hbm, k_hbm, v_hbm, a_hbm, h_hbm, dw_hbm, uw_hbm,
    down_out, up_out, bias_out,
    kv, sink, bb, w0, w1, q_s, a_s, h_s, o_s, t_s, kt, ve, mask,
    g0, g1, rc0, rc1, ra0, ra1, s20, s21, rb0, rb1, s3, r3, fin,
    bg, bgz, bgs, bgx, bgf,
    ld, kv_s, kv_r, sk_s, sk_r, bb_sr, w_sr, rs_sr, bg_sr,
):
    dp, ctx = lax.axis_index("dp"), lax.axis_index("ctx")
    y, c, x, z = dp // 2, dp % 2, ctx // NZ, ctx % NZ

    def dev(x_=x, y_=y, z_=z, c_=c):
        return (y_ * 2 + c_, x_ * NZ + z_)

    def off(v, i, n):
        return lax.rem(v + i + n, n)

    right, left = (dp, off(ctx, 1, N_CTX)), (dp, off(ctx, -1, N_CTX))
    jump = (dp, off(ctx, NZ, N_CTX))
    sent = []

    def rcopy(src, dst, send, recv, device):
        return pltpu.make_async_remote_copy(
            src_ref=src, dst_ref=dst, send_sem=send, recv_sem=recv, device_id=device, device_id_type=MESH
        )

    def push(src, dst, send, recv, device):
        copy = rcopy(src, dst, send, recv, device)
        copy.start()
        sent.append(copy)

    def arrived(dst, send, recv):
        rcopy(dst, dst, send, recv, right).wait_recv()

    loads = []
    for g in range(KV_HEADS):
        cols = pl.ds(g * HEAD_DIM, HEAD_DIM)
        loads.append(pltpu.make_async_copy(k_hbm.at[0, :, cols], kv.at[0, g, :, pl.ds(0, HEAD_DIM)], ld.at[2 * g]))
        loads.append(
            pltpu.make_async_copy(v_hbm.at[0, :, cols], kv.at[0, g, :, pl.ds(HEAD_DIM, HEAD_DIM)], ld.at[2 * g + 1])
        )
    own = (w0.at[c, y, x, z], w1.at[c, x, y, z])
    for half in range(2):
        rows = pl.multiple_of(dp * 2 * UP_ROWS + half * UP_ROWS, UP_ROWS)
        loads.append(
            pltpu.make_async_copy(uw_hbm.at[pl.ds(rows, UP_ROWS), :], own[half].at[pl.ds(0, UP_ROWS), :], ld.at[8 + half])
        )
        rows = pl.multiple_of(dp % 4 * 2 * DOWN_ROWS + half * DOWN_ROWS, DOWN_ROWS)
        cols = pl.multiple_of(dp // 4 * HEAD_DIM, HEAD_DIM)
        loads.append(
            pltpu.make_async_copy(
                dw_hbm.at[pl.ds(rows, DOWN_ROWS), pl.ds(cols, HEAD_DIM)],
                own[half].at[pl.ds(UP_ROWS, DOWN_ROWS), :],
                ld.at[10 + half],
            )
        )
    late = [
        pltpu.make_async_copy(q_hbm.at[0], q_s, ld.at[12]),
        pltpu.make_async_copy(a_hbm.at[0], a_s, ld.at[13]),
        pltpu.make_async_copy(h_hbm.at[0], h_s, ld.at[14]),
    ]
    for copy in loads + late:
        copy.start()

    barrier = pltpu.get_barrier_semaphore()
    partners = [left, right]
    partners += [dev(x_=off(x, i, NX)) for i in range(1, NX)]
    partners += [dev(z_=off(z, i, NZ)) for i in range(1, NZ)]
    partners += [(off(dp, i, N_DP), ctx) for i in range(1, N_DP)]
    for partner in partners:
        pl.semaphore_signal(barrier, inc=1, device_id=partner, device_id_type=MESH)
    row8 = lax.broadcasted_iota(jnp.int32, (8, HEAD_DIM), 0)
    bb[x, z] = jnp.where(row8 == 1, bias_ref[1], bias_ref[0]) * LOG2E
    for copy in loads:
        copy.wait()

    @pl.when(ctx == 0)
    def _():
        for g in range(KV_HEADS):
            sink[g] = kv[0, g, 0:SINKS, :]

    pl.semaphore_wait(barrier, len(partners))

    def kv_push(g, src, dst, device):
        push(kv.at[src, g], kv.at[dst, g], kv_s.at[dst, g], kv_r.at[dst, g], device)

    def kv_arrived(g, slot):
        arrived(kv.at[slot, g], kv_s.at[slot, g], kv_r.at[slot, g])

    for g in range(KV_HEADS):
        kv_push(g, 0, 1, right)
        kv_push(g, 0, 8, jump)

    def sink_copies(axis):
        if axis == "x":
            return [rcopy(sink, sink, sk_s.at[i], sk_r.at[0], dev(x_=off(x, i, NX))) for i in range(1, NX)]
        return [rcopy(sink, sink, sk_s.at[NX + i], sk_r.at[0], dev(z_=off(z, i, NZ))) for i in range(1, NZ)]

    @pl.when(ctx == 0)
    def _():
        for copy in sink_copies("x"):
            copy.start()

    for i in range(1, NZ):
        there = dev(z_=off(z, i, NZ))
        push(bb.at[x, z], bb.at[x, z], bb_sr.at[0, i], bb_sr.at[1, i], there)
        push(own[0], own[0], w_sr.at[0, i], w_sr.at[1, i], there)
        push(own[1], own[1], w_sr.at[0, NZ + i], w_sr.at[1, NZ + i], there)

    @pl.when(ctx != 0)
    def _():
        arrived(sink, sk_s.at[0], sk_r.at[0])

    @pl.when(z == 0)
    def _():
        for copy in sink_copies("z"):
            copy.start()

    def kv_hop(step):
        for g in range(KV_HEADS):
            kv_arrived(g, step)
            kv_push(g, step, step + 1, right)
            kv_arrived(g, 9 - step)
            kv_push(g, 9 - step, 8 - step, left)

    kv_hop(1)

    for i in range(1, NZ):
        frm = off(z, -i, NZ)
        arrived(bb.at[x, frm], bb_sr.at[0, i], bb_sr.at[1, i])
        arrived(w0.at[c, y, x, frm], w_sr.at[0, i], w_sr.at[1, i])
        arrived(w1.at[c, x, y, frm], w_sr.at[0, NZ + i], w_sr.at[1, NZ + i])
    for i in range(1, NX):
        to_x, to_y = dev(x_=off(x, i, NX)), dev(y_=off(y, i, NY))
        push(bb.at[x], bb.at[x], bb_sr.at[0, NZ + i], bb_sr.at[1, NZ + i], to_x)
        push(w0.at[c, y, x], w0.at[c, y, x], w_sr.at[0, 16 + i], w_sr.at[1, 16 + i], to_x)
        push(w1.at[c, x, y], w1.at[c, x, y], w_sr.at[0, 20 + i], w_sr.at[1, 20 + i], to_y)

    kv_hop(2)

    for i in range(1, NX):
        from_x, from_y = off(x, -i, NX), off(y, -i, NY)
        arrived(bb.at[from_x], bb_sr.at[0, NZ + i], bb_sr.at[1, NZ + i])
        arrived(w0.at[c, y, from_x], w_sr.at[0, 16 + i], w_sr.at[1, 16 + i])
        arrived(w1.at[c, x, from_y], w_sr.at[0, 20 + i], w_sr.at[1, 20 + i])
    for i in range(1, NX):
        to_x, to_y = dev(x_=off(x, i, NX)), dev(y_=off(y, i, NY))
        push(w0.at[c, y], w0.at[c, y], w_sr.at[0, 24 + i], w_sr.at[1, 24 + i], to_y)
        push(w1.at[c, x], w1.at[c, x], w_sr.at[0, 28 + i], w_sr.at[1, 28 + i], to_x)

    kv_hop(3)

    window, count = win_ref[0], cnt_ref[0]
    row = lax.broadcasted_iota(jnp.int32, (TOK, TOK), 0)
    col = lax.broadcasted_iota(jnp.int32, (TOK, TOK), 1)
    causal = col <= row

    def seen(block):
        return (block * TOK + row - col < window) & ((ctx - block) * TOK + col >= count)

    for j in range(7):
        mask[:, j * TOK : (j + 1) * TOK] = jnp.where(seen(ORDER[j]), 0.0, MASKED)
    both = jnp.where(causal, jnp.where(seen(0), 1, 0), jnp.where(seen(8), 1, 0)) == 1
    mask[:, MAIN : MAIN + TOK] = jnp.where(both, 0.0, MASKED)
    sink_seen = (col <= ctx * TOK + row) & (col < count)
    mask[:, MAIN + TOK : MAIN + 2 * TOK] = jnp.where(sink_seen, 0.0, MASKED)
    ve[:, HEAD_DIM:] = jnp.ones((COLS, HEAD_DIM), BF16)
    ve[BLOCKS * TOK :, 0:HEAD_DIM] = jnp.zeros((TOK, HEAD_DIM), BF16)
    bg[...] = jnp.zeros(bg.shape, F32)

    core_w = [
        rcopy(w.at[c], w.at[c], w_sr.at[0, 32 + half], w_sr.at[1, 32 + half], dev(c_=1 - c))
        for half, w in enumerate((w0, w1))
    ]

    late[0].wait()

    def attend_group(g, carry):
        for slot in range(4, 6):
            kv_arrived(g, slot)
        for j, block in enumerate(ORDER):
            kt[:, j * TOK : (j + 1) * TOK] = kv[block, g, :, 0:HEAD_DIM].T
            ve[j * TOK : (j + 1) * TOK, 0:HEAD_DIM] = kv[block, g, :, HEAD_DIM:]
        padded = jnp.concatenate(
            [sink[g, :, 0:HEAD_DIM], jnp.zeros((TOK - SINKS, HEAD_DIM), BF16)], axis=0
        )
        kt[:, BLOCKS * TOK :] = padded.T
        ve[BLOCKS * TOK : BLOCKS * TOK + SINKS, 0:HEAD_DIM] = sink[g, :, HEAD_DIM:]

        def attend_heads(step, carry):
            first = g * GROUP + step * HEAD_STEP
            rows = HEAD_STEP * TOK

            def columns(e):
                return pl.ds(pl.multiple_of((first + e) * HEAD_DIM, HEAD_DIM), HEAD_DIM)

            queries = jnp.concatenate([q_s[:, columns(e)] for e in range(HEAD_STEP)], axis=0)
            score = dot(queries, kt[...]) * SCORE_SCALE
            score = score.reshape(HEAD_STEP, TOK, COLS)
            parts = [
                score[:, :, j * TOK : (j + 1) * TOK] + mask[:, j * TOK : (j + 1) * TOK][None] for j in range(7)
            ]
            edge = jnp.where(causal[None], score[:, :, MAIN : MAIN + TOK], score[:, :, MAIN + TOK : MAIN + 2 * TOK])
            parts.append(edge + mask[:, MAIN : MAIN + TOK][None])
            biases = []
            for e in range(HEAD_STEP):
                head = first + e
                shard = head // 2
                biases.append(bb[shard // NZ, shard % NZ, e % 2 : e % 2 + 1, :])
            bias = jnp.concatenate([b[None] for b in biases], axis=0)
            parts.append(score[:, :, BLOCKS * TOK :] + (mask[:, MAIN + TOK : MAIN + 2 * TOK][None] + bias))
            top = parts[0]
            for part in parts[1:]:
                top = jnp.maximum(top, part)
            top = jnp.max(top, axis=-1, keepdims=True)
            probs = [jnp.exp2(part - top).astype(BF16) for part in parts]
            nothing = jnp.zeros((), BF16)
            near = jnp.where(causal[None], probs[7], nothing)
            far = jnp.where(causal[None], nothing, probs[7])
            local = jnp.concatenate(probs[:7] + [near, far], axis=-1).reshape(rows, BLOCKS * TOK)
            from_sinks = dot(probs[8].reshape(rows, TOK), ve[BLOCKS * TOK :, :])
            total = dot(local, ve[0 : BLOCKS * TOK, :]) + from_sinks
            scale = 1.0 / total[:, HEAD_DIM:]
            out = (total[:, 0:HEAD_DIM] * scale).astype(BF16)
            term = (from_sinks[:, 0:HEAD_DIM] - from_sinks[:, HEAD_DIM:] * out.astype(F32)) * scale
            for e in range(HEAD_STEP):
                o_s[:, columns(e)] = out[e * TOK : (e + 1) * TOK]
                t_s[:, columns(e)] = term[e * TOK : (e + 1) * TOK]
            return carry

        lax.fori_loop(0, GROUP // HEAD_STEP, attend_heads, 0)

        @pl.when(g == 0)
        def _():
            for i in range(1, NX):
                from_x, from_y = off(x, -i, NX), off(y, -i, NY)
                arrived(w0.at[c, from_y], w_sr.at[0, 24 + i], w_sr.at[1, 24 + i])
                arrived(w1.at[c, from_x], w_sr.at[0, 28 + i], w_sr.at[1, 28 + i])
            for copy in core_w:
                copy.start()

        return carry

    lax.fori_loop(0, KV_HEADS, attend_group, 0)

    arrived(w0.at[1 - c], w_sr.at[0, 32], w_sr.at[1, 32])
    arrived(w1.at[1 - c], w_sr.at[0, 33], w_sr.at[1, 33])
    late[1].wait()
    late[2].wait()

    pieces = [(p // 2, p % 2, half) for p in range(N_DP) for half in range(2)]

    def weight(xs, zs, piece, lo, hi):
        ys, cs, half = piece
        return w1[cs, xs, ys, zs, lo:hi, :] if half else w0[cs, ys, xs, zs, lo:hi, :]

    def low_grad_step(s, total):
        xs, zs = s // NZ, s % NZ
        up = jnp.concatenate([weight(xs, zs, piece, 0, UP_ROWS) for piece in pieces], axis=0)
        return total + dot(a_s[:, pl.ds(pl.multiple_of(s * 512, 512), 512)], up)

    low_grad = lax.fori_loop(0, N_CTX, low_grad_step, jnp.zeros((TOK, RANK), F32))
    low_grad_t = low_grad.T.astype(BF16)
    low_grad = low_grad.astype(BF16)

    def put(xs, zs, piece, lo, hi, value):
        ys, cs, half = piece
        if half:
            g1[cs, xs, ys, zs, lo:hi, :] = value
        else:
            g0[cs, ys, xs, zs, lo:hi, :] = value

    def down_step(s, total):
        xs, zs = s // NZ, s % NZ
        cols = pl.ds(pl.multiple_of(s * 256, 256), 256)
        down = jnp.concatenate(
            [
                jnp.concatenate([weight(xs, zs, piece, UP_ROWS, CHUNK) for piece in pieces[8 * e : 8 * e + 8]], axis=0)
                for e in range(2)
            ],
            axis=1,
        )
        out = o_s[:, cols]
        head_total = (h_s[:, cols].astype(F32) + 2.0 * dot(low_grad, down)).astype(BF16)
        bias_terms = jnp.sum(head_total.astype(F32) * t_s[:, cols], axis=0, keepdims=True)
        for e in range(2):
            bg[zs, xs, e : e + 1, :] = bias_terms[:, e * HEAD_DIM : (e + 1) * HEAD_DIM]
        grad = (2.0 * dot(low_grad_t, out)).astype(BF16)
        for e in range(2):
            for n, piece in enumerate(pieces[8 * e : 8 * e + 8]):
                put(
                    xs, zs, piece, UP_ROWS, CHUNK,
                    grad[n * DOWN_ROWS : (n + 1) * DOWN_ROWS, e * HEAD_DIM : (e + 1) * HEAD_DIM],
                )
        return total + dot_nt(out, down)

    low_out = lax.fori_loop(0, N_CTX, down_step, jnp.zeros((TOK, RANK), F32))
    low_out_t = low_out.T.astype(BF16)

    for i in range(1, NZ):
        push(bg.at[off(z, i, NZ)], bgz.at[i - 1], bg_sr.at[0, i], bg_sr.at[1, i], dev(z_=off(z, i, NZ)))

    def up_step(s, carry):
        xs, zs = s // NZ, s % NZ
        grad = (2.0 * dot(low_out_t, a_s[:, pl.ds(pl.multiple_of(s * 512, 512), 512)])).astype(BF16)
        for p in range(N_DP):
            for half in range(2):
                for j in range(2):
                    cols = 256 * half + 128 * j
                    put(
                        xs, zs, (p // 2, p % 2, half), 16 * j, 16 * j + 16,
                        grad[16 * p : 16 * p + 16, cols : cols + 128],
                    )
        return carry

    lax.fori_loop(0, N_CTX, up_step, 0)

    sibling = dev(c_=1 - c)
    push(g0.at[1 - c], rc0, rs_sr.at[0, 0], rs_sr.at[1, 0], sibling)
    push(g1.at[1 - c], rc1, rs_sr.at[0, 1], rs_sr.at[1, 1], sibling)

    for i in range(1, NZ):
        arrived(bgz.at[i - 1], bg_sr.at[0, i], bg_sr.at[1, i])
    terms = bg[z]
    for i in range(1, NZ):
        terms = terms + bgz[i - 1]
    bgs[...] = terms
    for i in range(1, NX):
        push(bgs.at[off(x, i, NX)], bgx.at[i - 1], bg_sr.at[0, NZ + i], bg_sr.at[1, NZ + i], dev(x_=off(x, i, NX)))

    def add_core(part, grads, received, first, second):
        arrived(received, rs_sr.at[0, part], rs_sr.at[1, part])

        def one(n, carry):
            a, b = n // second, n % second
            grads[c, a, b] = (grads[c, a, b].astype(F32) + received[a, b].astype(F32)).astype(BF16)
            return carry

        lax.fori_loop(0, first * second, one, 0)

    add_core(0, g0, rc0, NY, NX)
    for i in range(1, NY):
        push(g0.at[c, off(y, i, NY)], ra0.at[i - 1], rs_sr.at[0, 4 + i], rs_sr.at[1, 4 + i], dev(y_=off(y, i, NY)))
    add_core(1, g1, rc1, NX, NY)
    for i in range(1, NX):
        push(g1.at[c, off(x, i, NX)], ra1.at[i - 1], rs_sr.at[0, 8 + i], rs_sr.at[1, 8 + i], dev(x_=off(x, i, NX)))

    for i in range(1, NX):
        arrived(bgx.at[i - 1], bg_sr.at[0, NZ + i], bg_sr.at[1, NZ + i])
    terms = bgs[x]
    for i in range(1, NX):
        terms = terms + bgx[i - 1]
    bgf[dp] = terms
    for i in range(1, N_DP):
        push(bgf.at[dp], bgf.at[dp], bg_sr.at[0, 12 + i], bg_sr.at[1, 12 + i], (off(dp, i, N_DP), ctx))

    def add_three(grads, mine, received, result, base):
        for i in range(1, 4):
            arrived(received.at[i - 1], rs_sr.at[0, base + i], rs_sr.at[1, base + i])

        def one(n, carry):
            total = grads[c, mine, n].astype(F32)
            for i in range(3):
                total = total + received[i, n].astype(F32)
            result[n] = total.astype(BF16)
            return carry

        lax.fori_loop(0, 4, one, 0)

    add_three(g0, y, ra0, s20, 4)
    for i in range(1, NX):
        push(s20.at[off(x, i, NX)], rb0.at[i - 1], rs_sr.at[0, 12 + i], rs_sr.at[1, 12 + i], dev(x_=off(x, i, NX)))
    add_three(g1, x, ra1, s21, 8)
    for i in range(1, NY):
        push(s21.at[off(y, i, NY)], rb1.at[i - 1], rs_sr.at[0, 16 + i], rs_sr.at[1, 16 + i], dev(y_=off(y, i, NY)))

    for half, (mine, held, received) in enumerate(((x, s20, rb0), (y, s21, rb1))):
        for i in range(1, 4):
            arrived(received.at[i - 1], rs_sr.at[0, 12 + 4 * half + i], rs_sr.at[1, 12 + 4 * half + i])
        total = held[mine].astype(F32)
        for i in range(3):
            total = total + received[i].astype(F32)
        s3[:, half] = total.astype(BF16)
    for i in range(1, NZ):
        push(s3.at[off(z, i, NZ)], r3.at[i - 1], rs_sr.at[0, 20 + i], rs_sr.at[1, 20 + i], dev(z_=off(z, i, NZ)))
    for i in range(1, NZ):
        arrived(r3.at[i - 1], rs_sr.at[0, 20 + i], rs_sr.at[1, 20 + i])
    total = s3[z].astype(F32)
    for i in range(1, NZ):
        total = total + r3[i - 1].astype(F32)
    fin[dp] = total
    for i in range(1, N_DP):
        push(fin.at[dp], fin.at[dp], rs_sr.at[0, 28 + i], rs_sr.at[1, 28 + i], (off(dp, i, N_DP), ctx))

    for i in range(1, N_DP):
        frm = off(dp, -i, N_DP)
        arrived(bgf.at[frm], bg_sr.at[0, 12 + i], bg_sr.at[1, 12 + i])
    terms = bgf[0]
    for p in range(1, N_DP):
        terms = terms + bgf[p]
    bias_out[0] = jnp.sum(terms[0:1, :])
    bias_out[1] = jnp.sum(terms[1:2, :])

    for i in range(1, N_DP):
        frm = off(dp, -i, N_DP)
        arrived(fin.at[frm], rs_sr.at[0, 28 + i], rs_sr.at[1, 28 + i])
    for b in range(4):
        block = jnp.concatenate([fin[p, b // 2, 16 * (b % 2) : 16 * (b % 2) + 16, :] for p in range(N_DP)], axis=0)
        up_out[128 * b : 128 * b + 128, :] = block.T
    for e in range(2):
        block = jnp.concatenate(
            [fin[4 * e + n // 2, n % 2, UP_ROWS:CHUNK, :] for n in range(8)], axis=0
        )
        down_out[:, e * HEAD_DIM : (e + 1) * HEAD_DIM] = block

    for copy in sent + core_w:
        copy.wait_send()

    @pl.when(ctx == 0)
    def _():
        for copy in sink_copies("x"):
            copy.wait_send()

    @pl.when(z == 0)
    def _():
        for copy in sink_copies("z"):
            copy.wait_send()


def on_device(q, k, v, a, h, bias, windows, counts, down, up):
    hbm, smem, vmem = (pl.BlockSpec(memory_space=s) for s in (pl.ANY, pltpu.SMEM, pltpu.VMEM))
    sem = pltpu.SemaphoreType.DMA
    chunk = (CHUNK, HEAD_DIM)
    heads = HEADS * HEAD_DIM
    scratch = [
        pltpu.VMEM((BLOCKS, KV_HEADS, TOK, 2 * HEAD_DIM), BF16),
        pltpu.VMEM((KV_HEADS, SINKS, 2 * HEAD_DIM), BF16),
        pltpu.VMEM((NX, NZ, 8, HEAD_DIM), F32),
        pltpu.VMEM((2, NY, NX, NZ) + chunk, BF16),
        pltpu.VMEM((2, NX, NY, NZ) + chunk, BF16),
        pltpu.VMEM((TOK, heads), BF16),
        pltpu.VMEM((TOK, a.shape[2]), BF16),
        pltpu.VMEM((TOK, heads), BF16),
        pltpu.VMEM((TOK, heads), BF16),
        pltpu.VMEM((TOK, heads), F32),
        pltpu.VMEM((HEAD_DIM, COLS), BF16),
        pltpu.VMEM((COLS, 2 * HEAD_DIM), BF16),
        pltpu.VMEM((TOK, BLOCKS * TOK), F32),
        pltpu.VMEM((2, NY, NX, NZ) + chunk, BF16),
        pltpu.VMEM((2, NX, NY, NZ) + chunk, BF16),
        pltpu.VMEM((NY, NX, NZ) + chunk, BF16),
        pltpu.VMEM((NX, NY, NZ) + chunk, BF16),
        pltpu.VMEM((3, NX, NZ) + chunk, BF16),
        pltpu.VMEM((3, NY, NZ) + chunk, BF16),
        pltpu.VMEM((NX, NZ) + chunk, BF16),
        pltpu.VMEM((NY, NZ) + chunk, BF16),
        pltpu.VMEM((3, NZ) + chunk, BF16),
        pltpu.VMEM((3, NZ) + chunk, BF16),
        pltpu.VMEM((NZ, 2) + chunk, BF16),
        pltpu.VMEM((NZ - 1, 2) + chunk, BF16),
        pltpu.VMEM((N_DP, 2) + chunk, F32),
        pltpu.VMEM((NZ, NX, 8, HEAD_DIM), F32),
        pltpu.VMEM((NZ - 1, NX, 8, HEAD_DIM), F32),
        pltpu.VMEM((NX, 8, HEAD_DIM), F32),
        pltpu.VMEM((NX - 1, 8, HEAD_DIM), F32),
        pltpu.VMEM((N_DP, 8, HEAD_DIM), F32),
        sem((15,)),
        sem((BLOCKS, KV_HEADS)),
        sem((BLOCKS, KV_HEADS)),
        sem((NX + NZ,)),
        sem((1,)),
        sem((2, NZ + NX)),
        sem((2, 34)),
        sem((2, 36)),
        sem((2, 20)),
    ]
    return pl.pallas_call(
        kernel,
        out_shape=(
            jax.ShapeDtypeStruct(down.shape, F32),
            jax.ShapeDtypeStruct(up.shape, F32),
            jax.ShapeDtypeStruct(bias.shape, F32),
        ),
        in_specs=[smem] * 3 + [hbm] * 7,
        out_specs=(vmem, vmem, smem),
        scratch_shapes=scratch,
        compiler_params=pltpu.CompilerParams(
            collective_id=0, has_side_effects=True, vmem_limit_bytes=60 * 1024 * 1024
        ),
        name="token_parallel",
    )(bias, windows, counts, q, k, v, a, h, down, up)


def solution(mesh):
    rows = P("dp", "ctx", None)
    placed = (rows,) * 5 + (P("ctx"), P("dp"), P("dp"), P(None, "ctx"), P("ctx", None))
    return jax.shard_map(
        on_device,
        mesh=mesh,
        in_specs=placed,
        out_specs=(P(None, "ctx"), P("ctx", None), P("ctx")),
        check_vma=False,
    )
```

```python
import jax
import jax.numpy as jnp
from jax import lax
from jax.experimental import pallas as pl
from jax.experimental.pallas import tpu as pltpu
from jax.sharding import PartitionSpec as P

NX, NY, NZ = 4, 4, 8
N_CTX, N_DP = NX * NZ, NY * 2
TOK = 128
HEAD_DIM = 128
KV_HEADS = 4
GROUP = 16
HEADS = KV_HEADS * GROUP
RANK = 128
SINKS = 16
BLOCKS = 9
UP_ROWS, DOWN_ROWS = 32, 16
HEAD_STEP = 4
MASKED = -1e30
LOG2E = 1.4426950408889634
SCORE_SCALE = LOG2E * HEAD_DIM**-0.5
BF16, F32 = jnp.bfloat16, jnp.float32
MESH = pl.DeviceIdType.MESH

ORDER = (1, 2, 3, 4, 5, 6, 7, 0, 8)
MAIN = 7 * TOK
COLS = 10 * TOK


def dot(a, b):
    return lax.dot_general(a, b, (((1,), (0,)), ((), ())), preferred_element_type=F32)


def dot_nt(a, b):
    return lax.dot_general(a, b, (((1,), (1,)), ((), ())), preferred_element_type=F32)


def kernel(
    bias_ref, win_ref, cnt_ref, q_hbm, k_hbm, v_hbm, a_hbm, h_hbm, dw_hbm, uw_hbm,
    fin_u_out, fin_d_out, bias_out,
    kv, sink, bb, wu, wd, q_s, a_s, h_s, o_s, t_s, kt, ve, mask,
    gu, gd, rcu, rcd, rau, rad, s2u, s2d, rbu, rbd, s3u, s3d, r3u, r3d, finu, find,
    bg, bgz, bgs, bgx, bgf,
    ld, kv_s, kv_r, sk, bb_s, bb_r, w_s, w_r, rs_s, rs_r, bg_s, bg_r,
):
    dp, ctx = lax.axis_index("dp"), lax.axis_index("ctx")
    y, c, x, z = dp // 2, dp % 2, ctx // NZ, ctx % NZ

    def dev(x_=x, y_=y, z_=z, c_=c):
        return (y_ * 2 + c_, x_ * NZ + z_)

    def off(v, i, n):
        return lax.rem(v + i + n, n)

    right, left = (dp, off(ctx, 1, N_CTX)), (dp, off(ctx, -1, N_CTX))
    jump = (dp, off(ctx, NZ, N_CTX))
    sibling = dev(c_=1 - c)

    def rcopy(src, dst, send, recv, device):
        return pltpu.make_async_remote_copy(
            src_ref=src, dst_ref=dst, send_sem=send, recv_sem=recv, device_id=device, device_id_type=MESH
        )

    def push(src, dst, send, recv, device):
        rcopy(src, dst, send, recv, device).start()

    def arrived(ref, recv):
        rcopy(ref, ref, recv, recv, right).wait_recv()

    def left_here(ref, send):
        rcopy(ref, ref, send, send, right).wait_send()

    for g in range(KV_HEADS):
        cols = pl.ds(g * HEAD_DIM, HEAD_DIM)
        pltpu.make_async_copy(k_hbm.at[0, :, cols], kv.at[0, g, :, pl.ds(0, HEAD_DIM)], ld.at[0]).start()
        pltpu.make_async_copy(v_hbm.at[0, :, cols], kv.at[0, g, :, pl.ds(HEAD_DIM, HEAD_DIM)], ld.at[0]).start()
    for half in range(2):
        rows = pl.multiple_of(dp % 4 * 2 * DOWN_ROWS + half * DOWN_ROWS, DOWN_ROWS)
        cols = pl.multiple_of(dp // 4 * HEAD_DIM, HEAD_DIM)
        pltpu.make_async_copy(
            dw_hbm.at[pl.ds(rows, DOWN_ROWS), pl.ds(cols, HEAD_DIM)], wd.at[half, c, x, y, z], ld.at[1]
        ).start()
        rows = pl.multiple_of(dp * 2 * UP_ROWS + half * UP_ROWS, UP_ROWS)
        pltpu.make_async_copy(uw_hbm.at[pl.ds(rows, UP_ROWS), :], wu.at[half, c, x, y, z], ld.at[2]).start()
    late = [
        pltpu.make_async_copy(q_hbm.at[0], q_s, ld.at[3]),
        pltpu.make_async_copy(a_hbm.at[0], a_s, ld.at[4]),
        pltpu.make_async_copy(h_hbm.at[0], h_s, ld.at[5]),
    ]
    for copy in late:
        copy.start()

    barrier = pltpu.get_barrier_semaphore()
    partners = [left, right]
    partners += [dev(x_=off(x, i, NX)) for i in range(1, NX)]
    partners += [dev(z_=off(z, i, NZ)) for i in range(1, NZ)]
    partners += [(off(dp, i, N_DP), ctx) for i in range(1, N_DP)]
    for partner in partners:
        pl.semaphore_signal(barrier, inc=1, device_id=partner, device_id_type=MESH)
    row8 = lax.broadcasted_iota(jnp.int32, (8, HEAD_DIM), 0)
    bb[x, z] = jnp.where(row8 == 1, bias_ref[1], bias_ref[0]) * LOG2E
    for n, ref in enumerate((kv.at[0], wd.at[:, c, x, y, z], wu.at[:, c, x, y, z])):
        pltpu.make_async_copy(ref, ref, ld.at[n]).wait()

    @pl.when(ctx == 0)
    def _():
        for g in range(KV_HEADS):
            sink[g] = kv[0, g, 0:SINKS, :]

    pl.semaphore_wait(barrier, len(partners))

    first_z = z == 0
    far_slot = jnp.where(first_z, 7, 8)
    far_device = (dp, jnp.where(first_z, x * NZ + NZ - 1, off(ctx, NZ, N_CTX)))

    def kv_push(g, src, dst, device):
        push(kv.at[src, g], kv.at[dst, g], kv_s.at[0], kv_r.at[dst, g], device)

    def kv_arrived(g, slot):
        arrived(kv.at[slot, g], kv_r.at[slot, g])

    def kv_hop(step):
        for g in range(KV_HEADS):
            kv_arrived(g, step)
            kv_push(g, step, step + 1, right)
            if step == 1:

                @pl.when(z != 0)
                def _():
                    kv_arrived(g, 8)
                    kv_push(g, 8, 7, left)

            else:
                kv_arrived(g, 9 - step)
                kv_push(g, 9 - step, 8 - step, left)

    for g in range(KV_HEADS):
        kv_push(g, 0, 1, right)
        kv_push(g, 0, far_slot, far_device)

    def sink_copies(axis):
        if axis == "x":
            return [rcopy(sink, sink, sk.at[0], sk.at[2], dev(x_=off(x, i, NX))) for i in range(1, NX)]
        return [rcopy(sink, sink, sk.at[1], sk.at[2], dev(z_=off(z, i, NZ))) for i in range(1, NZ)]

    @pl.when(ctx == 0)
    def _():
        for copy in sink_copies("x"):
            copy.start()

    weights = (wd, wu)

    def w_push(part, stage, src, device):
        push(src, src, w_s.at[part, stage], w_r.at[part, stage], device)

    w_sizes = [
        (w.at[0, c, 0, pl.ds(0, 2), pl.ds(0, 7)], w.at[0, c, pl.ds(0, 3), pl.ds(0, 2)], w.at[:, c, pl.ds(0, 3)], w.at[:, c])
        for w in weights
    ]

    def w_arrived(part, stage):
        arrived(w_sizes[part][stage], w_r.at[part, stage])

    def along_z(part):
        for i in range(1, NZ):
            w_push(part, 0, weights[part].at[:, c, x, y, z], dev(z_=off(z, i, NZ)))

    def second(part):
        w = weights[part]
        for i in range(1, NX):
            if part == 0:
                w_push(part, 1, w.at[:, c, x, y], dev(x_=off(x, i, NX)))
            else:
                w_push(part, 1, w.at[0, c, x, y], dev(x_=off(x, i, NX)))
                w_push(part, 1, w.at[1, c, x, y], dev(y_=off(y, i, NY)))

    def third(part, half):
        w = weights[part]
        for i in range(1, NX):
            if part == 1 and half == 1:
                w_push(part, 2, w.at[1, c, x], dev(x_=off(x, i, NX)))
            else:
                w_push(part, 2, w.at[half, c, :, y], dev(y_=off(y, i, NY)))

    def core(part):
        w_push(part, 3, weights[part].at[:, c], sibling)

    for i in range(1, NZ):
        push(bb.at[x, z], bb.at[x, z], bb_s.at[0], bb_r.at[0], dev(z_=off(z, i, NZ)))
    along_z(0)
    along_z(1)

    window, count = win_ref[0], cnt_ref[0]
    row = lax.broadcasted_iota(jnp.int32, (TOK, TOK), 0)
    col = lax.broadcasted_iota(jnp.int32, (TOK, TOK), 1)
    causal = col <= row

    def seen(block):
        return (block * TOK + row - col < window) & ((ctx - block) * TOK + col >= count)

    for j in range(7):
        mask[:, j * TOK : (j + 1) * TOK] = jnp.where(seen(ORDER[j]), 0.0, MASKED)
    both = jnp.where(causal, jnp.where(seen(0), 1, 0), jnp.where(seen(8), 1, 0)) == 1
    mask[:, MAIN : MAIN + TOK] = jnp.where(both, 0.0, MASKED)
    sink_seen = (col <= ctx * TOK + row) & (col < count)
    mask[:, MAIN + TOK : MAIN + 2 * TOK] = jnp.where(sink_seen, 0.0, MASKED)
    ve[:, HEAD_DIM:] = jnp.ones((COLS, HEAD_DIM), BF16)
    ve[BLOCKS * TOK :, 0:HEAD_DIM] = jnp.zeros((TOK, HEAD_DIM), BF16)
    bg[...] = jnp.zeros(bg.shape, F32)

    kv_hop(1)

    @pl.when((z == 0) & (x != 0))
    def _():
        arrived(sink, sk.at[2])

    @pl.when(z == 0)
    def _():
        for copy in sink_copies("z"):
            copy.start()

    arrived(bb.at[0, pl.ds(0, 7)], bb_r.at[0])
    for i in range(1, NX):
        push(bb.at[x], bb.at[x], bb_s.at[1], bb_r.at[1], dev(x_=off(x, i, NX)))
    w_arrived(0, 0)
    second(0)

    kv_hop(2)

    w_arrived(1, 0)
    second(1)
    w_arrived(0, 1)
    third(0, 0)
    third(0, 1)

    kv_hop(3)

    @pl.when(first_z)
    def _():
        for g in range(KV_HEADS):
            kv_push(g, 0, 8, jump)

    w_arrived(1, 1)
    third(1, 0)
    arrived(bb.at[pl.ds(0, 3)], bb_r.at[1])

    @pl.when(z != 0)
    def _():
        arrived(sink, sk.at[2])

    late[0].wait()

    def attend_group(g, carry):
        kv_arrived(g, 4)
        kv_arrived(g, 5)

        @pl.when(first_z)
        def _():
            kv_arrived(g, 8)

        for j, block in enumerate(ORDER):
            kt[:, j * TOK : (j + 1) * TOK] = kv[block, g, :, 0:HEAD_DIM].T
            ve[j * TOK : (j + 1) * TOK, 0:HEAD_DIM] = kv[block, g, :, HEAD_DIM:]
        padded = jnp.concatenate(
            [sink[g, :, 0:HEAD_DIM], jnp.zeros((TOK - SINKS, HEAD_DIM), BF16)], axis=0
        )
        kt[:, BLOCKS * TOK :] = padded.T
        ve[BLOCKS * TOK : BLOCKS * TOK + SINKS, 0:HEAD_DIM] = sink[g, :, HEAD_DIM:]

        def attend_heads(step, carry):
            first = g * GROUP + step * HEAD_STEP
            rows = HEAD_STEP * TOK

            def columns(e):
                return pl.ds(pl.multiple_of((first + e) * HEAD_DIM, HEAD_DIM), HEAD_DIM)

            queries = jnp.concatenate([q_s[:, columns(e)] for e in range(HEAD_STEP)], axis=0)
            score = dot(queries, kt[...]) * SCORE_SCALE
            score = score.reshape(HEAD_STEP, TOK, COLS)
            parts = [
                score[:, :, j * TOK : (j + 1) * TOK] + mask[:, j * TOK : (j + 1) * TOK][None] for j in range(7)
            ]
            edge = jnp.where(causal[None], score[:, :, MAIN : MAIN + TOK], score[:, :, MAIN + TOK : MAIN + 2 * TOK])
            parts.append(edge + mask[:, MAIN : MAIN + TOK][None])
            biases = []
            for e in range(HEAD_STEP):
                head = first + e
                shard = head // 2
                biases.append(bb[shard // NZ, shard % NZ, e % 2 : e % 2 + 1, :])
            bias = jnp.concatenate([b[None] for b in biases], axis=0)
            parts.append(score[:, :, BLOCKS * TOK :] + (mask[:, MAIN + TOK : MAIN + 2 * TOK][None] + bias))
            top = parts[0]
            for part in parts[1:]:
                top = jnp.maximum(top, part)
            top = jnp.max(top, axis=-1, keepdims=True)
            probs = [jnp.exp2(part - top).astype(BF16) for part in parts]
            nothing = jnp.zeros((), BF16)
            near = jnp.where(causal[None], probs[7], nothing)
            far = jnp.where(causal[None], nothing, probs[7])
            local = jnp.concatenate(probs[:7] + [near, far], axis=-1).reshape(rows, BLOCKS * TOK)
            from_sinks = dot(probs[8].reshape(rows, TOK), ve[BLOCKS * TOK :, :])
            total = dot(local, ve[0 : BLOCKS * TOK, :]) + from_sinks
            scale = 1.0 / total[:, HEAD_DIM:]
            out = (total[:, 0:HEAD_DIM] * scale).astype(BF16)
            term = (from_sinks[:, 0:HEAD_DIM] - from_sinks[:, HEAD_DIM:] * out.astype(F32)) * scale
            for e in range(HEAD_STEP):
                o_s[:, columns(e)] = out[e * TOK : (e + 1) * TOK]
                t_s[:, columns(e)] = term[e * TOK : (e + 1) * TOK]
            return carry

        lax.fori_loop(0, GROUP // HEAD_STEP, attend_heads, 0)

        @pl.when(g == 0)
        def _():
            third(1, 1)

        @pl.when(g == 2)
        def _():
            w_arrived(0, 2)
            core(0)

        return carry

    lax.fori_loop(0, KV_HEADS, attend_group, 0)

    pieces = [(half, p % 2, p // 2) for p in range(N_DP) for half in range(2)]

    def down_weight(xs, zs):
        return [
            jnp.concatenate([wd[half, cs, xs, ys, zs] for half, cs, ys in pieces[8 * e : 8 * e + 8]], axis=0)
            for e in range(2)
        ]

    w_arrived(0, 3)

    def low_out_step(xs, total):
        down = jnp.concatenate([w for zs in range(NZ) for w in down_weight(xs, zs)], axis=1)
        return total + dot_nt(down, o_s[:, pl.ds(pl.multiple_of(xs * 2048, 2048), 2048)])

    low_out_t = lax.fori_loop(0, NX, low_out_step, jnp.zeros((RANK, TOK), F32)).astype(BF16)
    late[1].wait()

    grads, from_core = (gd, gu), (rcd, rcu)
    first_in, first_sum = (rad, rau), (s2d, s2u)
    second_in, second_sum = (rbd, rbu), (s3d, s3u)
    third_in, final = (r3d, r3u), (find, finu)
    order = [off(x, i, NX) for i in (1, 2, 3, 0)]

    CORE, FIRST, SECOND, THIRD, LAST = 0, 4, 5, 6, 7
    rs_sizes = [
        {CORE: from_core[p], FIRST: first_in[p], SECOND: second_in[p], THIRD: third_in[p], LAST: final[p].at[pl.ds(0, 7)]}
        for p in range(2)
    ]

    def rs_push(part, stage, src, dst, device, row=0):
        push(src, dst, rs_s.at[part, stage], rs_r.at[part, stage + row], device)

    def rs_arrived(part, stage):
        arrived(rs_sizes[part][stage], rs_r.at[part, stage])

    def to_core(part, j):
        xs = order[j]
        rs_push(part, CORE, grads[part].at[:, 1 - c, xs], from_core[part].at[:, xs], sibling, j)

    def first_stage(part, j):
        xs = order[j]
        arrived(from_core[part].at[:, xs], rs_r.at[part, j])
        mine, theirs = grads[part], from_core[part]

        def one(n, carry):
            half, ys = n // NY, n % NY
            mine[half, c, xs, ys] = (mine[half, c, xs, ys].astype(F32) + theirs[half, xs, ys].astype(F32)).astype(BF16)
            return carry

        lax.fori_loop(0, 2 * NY, one, 0)
        for i in range(1, NY):
            rs_push(part, FIRST, mine.at[0, c, xs, off(y, i, NY)], first_in[part].at[0, i - 1, xs], dev(y_=off(y, i, NY)))
        if j < 3:
            rs_push(part, FIRST, mine.at[1, c, xs], first_in[part].at[1, j], dev(x_=xs))

    def second_stage(part):
        rs_arrived(part, FIRST)
        mine, theirs, total = grads[part], first_in[part], first_sum[part]

        def one(n, carry):
            for half, own in ((0, mine.at[0, c, n, y]), (1, mine.at[1, c, x, n])):
                acc = own[...].astype(F32)
                for i in range(3):
                    acc = acc + theirs[half, i, n].astype(F32)
                total[half, n] = acc.astype(BF16)
            return carry

        lax.fori_loop(0, 4, one, 0)
        for i in range(1, NX):
            to_x, to_y = off(x, i, NX), off(y, i, NY)
            rs_push(part, SECOND, total.at[0, to_x], second_in[part].at[0, i - 1], dev(x_=to_x))
            rs_push(part, SECOND, total.at[1, to_y], second_in[part].at[1, i - 1], dev(y_=to_y))

    def third_stage(part):
        rs_arrived(part, SECOND)
        mine, theirs, total = first_sum[part], second_in[part], second_sum[part]
        for half, own in ((0, x), (1, y)):
            acc = mine[half, own].astype(F32)
            for i in range(3):
                acc = acc + theirs[half, i].astype(F32)
            total[:, half] = acc.astype(BF16)
        for i in range(1, NZ):
            rs_push(part, THIRD, total.at[off(z, i, NZ)], third_in[part].at[i - 1], dev(z_=off(z, i, NZ)))

    def last_stage(part):
        rs_arrived(part, THIRD)
        acc = second_sum[part][z].astype(F32)
        for i in range(1, NZ):
            acc = acc + third_in[part][i - 1].astype(F32)
        final[part][dp] = acc.astype(BF16)
        for i in range(1, N_DP):
            rs_push(part, LAST, final[part].at[dp], final[part].at[dp], (off(dp, i, N_DP), ctx))

    def last_arrived(part):
        rs_arrived(part, LAST)

    def up_row(xs):
        def step(zs, carry):
            cols = pl.ds(pl.multiple_of((xs * NZ + zs) * 512, 512), 512)
            grad = (2.0 * dot(low_out_t, a_s[:, cols])).astype(BF16)
            for p in range(N_DP):
                for half in range(2):
                    for j in range(2):
                        lane = 256 * half + 128 * j
                        gu[half, p % 2, xs, p // 2, zs, 16 * j : 16 * j + 16, :] = grad[
                            16 * p : 16 * p + 16, lane : lane + 128
                        ]
            return carry

        lax.fori_loop(0, NZ, step, 0, unroll=2)

    for j in range(NX):
        up_row(order[j])
        to_core(1, j)
        if j > 0:
            first_stage(1, j - 1)
        if j == 2:
            w_arrived(1, 2)
            core(1)
    first_stage(1, 3)

    w_arrived(1, 3)

    def low_grad_step(xs, total):
        up = jnp.concatenate(
            [wu[half, cs, xs, ys, zs] for zs in range(NZ) for half, cs, ys in pieces], axis=0
        )
        return total + dot(a_s[:, pl.ds(pl.multiple_of(xs * 4096, 4096), 4096)], up)

    low_grad = lax.fori_loop(0, NX, low_grad_step, jnp.zeros((TOK, RANK), F32))
    low_grad_t = low_grad.T.astype(BF16)
    low_grad = low_grad.astype(BF16)
    late[2].wait()

    def down_row(xs):
        def step(zs, carry):
            cols = pl.ds(pl.multiple_of((xs * NZ + zs) * 256, 256), 256)
            down = jnp.concatenate(down_weight(xs, zs), axis=1)
            head_total = (h_s[:, cols].astype(F32) + 2.0 * dot(low_grad, down)).astype(BF16)
            bias_terms = jnp.sum(head_total.astype(F32) * t_s[:, cols], axis=0, keepdims=True)
            for e in range(2):
                bg[zs, xs, e : e + 1, :] = bias_terms[:, e * HEAD_DIM : (e + 1) * HEAD_DIM]
            grad = (2.0 * dot(low_grad_t, o_s[:, cols])).astype(BF16)
            for n, (half, cs, ys) in enumerate(pieces):
                e, r = n // 8, n % 8 * DOWN_ROWS
                gd[half, cs, xs, ys, zs] = grad[r : r + DOWN_ROWS, e * HEAD_DIM : (e + 1) * HEAD_DIM]
            return carry

        lax.fori_loop(0, NZ, step, 0, unroll=2)

    for j in range(NX):
        down_row(order[j])
        to_core(0, j)
        if j > 0:
            first_stage(0, j - 1)

    for i in range(1, NZ):
        push(bg.at[off(z, i, NZ)], bgz.at[i - 1], bg_s.at[0], bg_r.at[0], dev(z_=off(z, i, NZ)))
    first_stage(0, 3)
    second_stage(1)

    arrived(bgz, bg_r.at[0])
    terms = bg[z]
    for i in range(1, NZ):
        terms = terms + bgz[i - 1]
    bgs[...] = terms
    for i in range(1, NX):
        push(bgs.at[off(x, i, NX)], bgx.at[i - 1], bg_s.at[1], bg_r.at[1], dev(x_=off(x, i, NX)))

    second_stage(0)
    third_stage(1)

    arrived(bgx, bg_r.at[1])
    terms = bgs[x]
    for i in range(1, NX):
        terms = terms + bgx[i - 1]
    bgf[dp] = terms
    for i in range(1, N_DP):
        push(bgf.at[dp], bgf.at[dp], bg_s.at[2], bg_r.at[2], (off(dp, i, N_DP), ctx))

    third_stage(0)
    last_stage(1)
    last_stage(0)

    arrived(bgf.at[pl.ds(0, 7)], bg_r.at[2])
    terms = bgf[0]
    for p in range(1, N_DP):
        terms = terms + bgf[p]
    bias_out[...] = terms
    last_arrived(1)
    fin_u_out[...] = finu[...]
    last_arrived(0)
    fin_d_out[...] = find[...]

    left_here(kv.at[pl.ds(1, 8)], kv_s.at[0])
    left_here(bb.at[0, pl.ds(0, 7)], bb_s.at[0])
    left_here(bb.at[pl.ds(0, 3)], bb_s.at[1])
    for part in range(2):
        for stage in range(4):
            left_here(w_sizes[part][stage], w_s.at[part, stage])
        for stage, ref in rs_sizes[part].items():
            left_here(ref, rs_s.at[part, stage])
    left_here(bgz, bg_s.at[0])
    left_here(bgx, bg_s.at[1])
    left_here(bgf.at[pl.ds(0, 7)], bg_s.at[2])

    @pl.when(ctx == 0)
    def _():
        left_here(kv.at[0, :, pl.ds(0, 3 * SINKS), :], sk.at[0])

    @pl.when(z == 0)
    def _():
        left_here(kv.at[0, :, pl.ds(0, 7 * SINKS), :], sk.at[1])


def write_out(fin_u, fin_d, terms, down_out, up_out, bias_out):
    for b in range(4):
        block = jnp.concatenate([fin_u[p, b // 2, 16 * (b % 2) : 16 * (b % 2) + 16, :] for p in range(N_DP)], axis=0)
        up_out[128 * b : 128 * b + 128, :] = block.astype(F32).T
    for e in range(2):
        block = jnp.concatenate([fin_d[4 * e + n // 2, n % 2] for n in range(8)], axis=0)
        down_out[:, e * HEAD_DIM : (e + 1) * HEAD_DIM] = block.astype(F32)
    bias_out[0] = jnp.sum(terms[0:1, :])
    bias_out[1] = jnp.sum(terms[1:2, :])


def on_device(q, k, v, a, h, bias, windows, counts, down, up):
    hbm, smem, vmem = (pl.BlockSpec(memory_space=s) for s in (pl.ANY, pltpu.SMEM, pltpu.VMEM))
    sem = pltpu.SemaphoreType.DMA
    heads = HEADS * HEAD_DIM

    def pair(*dims):
        return [pltpu.VMEM(dims + (rows, HEAD_DIM), BF16) for rows in (UP_ROWS, DOWN_ROWS)]

    scratch = [
        pltpu.VMEM((BLOCKS, KV_HEADS, TOK, 2 * HEAD_DIM), BF16),
        pltpu.VMEM((KV_HEADS, SINKS, 2 * HEAD_DIM), BF16),
        pltpu.VMEM((NX, NZ, 8, HEAD_DIM), F32),
        *pair(2, 2, NX, NY, NZ),
        pltpu.VMEM((TOK, heads), BF16),
        pltpu.VMEM((TOK, a.shape[2]), BF16),
        pltpu.VMEM((TOK, heads), BF16),
        pltpu.VMEM((TOK, heads), BF16),
        pltpu.VMEM((TOK, heads), F32),
        pltpu.VMEM((HEAD_DIM, COLS), BF16),
        pltpu.VMEM((COLS, 2 * HEAD_DIM), BF16),
        pltpu.VMEM((TOK, BLOCKS * TOK), F32),
        *pair(2, 2, NX, NY, NZ),
        *pair(2, NX, NY, NZ),
        *pair(2, 3, 4, NZ),
        *pair(2, 4, NZ),
        *pair(2, 3, NZ),
        *pair(NZ, 2),
        *pair(NZ - 1, 2),
        *pair(N_DP, 2),
        pltpu.VMEM((NZ, NX, 8, HEAD_DIM), F32),
        pltpu.VMEM((NZ - 1, NX, 8, HEAD_DIM), F32),
        pltpu.VMEM((NX, 8, HEAD_DIM), F32),
        pltpu.VMEM((NX - 1, 8, HEAD_DIM), F32),
        pltpu.VMEM((N_DP, 8, HEAD_DIM), F32),
        sem((6,)),
        sem((1,)),
        sem((BLOCKS, KV_HEADS)),
        sem((3,)),
        sem((2,)),
        sem((2,)),
        sem((2, 4)),
        sem((2, 4)),
        sem((2, 8)),
        sem((2, 8)),
        sem((3,)),
        sem((3,)),
    ]
    reduced = pl.pallas_call(
        kernel,
        out_shape=(
            jax.ShapeDtypeStruct((N_DP, 2, UP_ROWS, HEAD_DIM), BF16),
            jax.ShapeDtypeStruct((N_DP, 2, DOWN_ROWS, HEAD_DIM), BF16),
            jax.ShapeDtypeStruct((8, HEAD_DIM), F32),
        ),
        in_specs=[smem] * 3 + [hbm] * 7,
        out_specs=(vmem, vmem, vmem),
        scratch_shapes=scratch,
        compiler_params=pltpu.CompilerParams(
            collective_id=0, has_side_effects=True, vmem_limit_bytes=60 * 1024 * 1024
        ),
        name="token_parallel",
    )(bias, windows, counts, q, k, v, a, h, down, up)
    return pl.pallas_call(
        write_out,
        out_shape=(
            jax.ShapeDtypeStruct(down.shape, F32),
            jax.ShapeDtypeStruct(up.shape, F32),
            jax.ShapeDtypeStruct(bias.shape, F32),
        ),
        in_specs=[vmem] * 3,
        out_specs=(vmem, vmem, smem),
        name="write_out",
    )(*reduced)


def solution(mesh):
    rows = P("dp", "ctx", None)
    placed = (rows,) * 5 + (P("ctx"), P("dp"), P("dp"), P(None, "ctx"), P("ctx", None))
    return jax.shard_map(
        on_device,
        mesh=mesh,
        in_specs=placed,
        out_specs=(P(None, "ctx"), P("ctx", None), P("ctx")),
        check_vma=False,
    )
```

```python
import jax
import jax.numpy as jnp
from jax import lax
from jax.experimental import pallas as pl
from jax.experimental.pallas import tpu as pltpu
from jax.sharding import PartitionSpec as P

NX, NY, NZ = 4, 4, 8
N_CTX, N_DP = NX * NZ, NY * 2
TOK = 128
HEAD_DIM = 128
KV_HEADS = 4
GROUP = 16
HEADS = KV_HEADS * GROUP
RANK = 128
SINKS = 16
BLOCKS = 9
UP_ROWS, DOWN_ROWS = 32, 16
HEAD_STEP = 4
MASKED = -1e30
LOG2E = 1.4426950408889634
SCORE_SCALE = LOG2E * HEAD_DIM**-0.5
BF16, F32 = jnp.bfloat16, jnp.float32
MESH = pl.DeviceIdType.MESH

ORDER = (1, 2, 3, 4, 5, 6, 7, 0, 8)
COLS = 10 * TOK


def dot(a, b):
    return lax.dot_general(a, b, (((1,), (0,)), ((), ())), preferred_element_type=F32)


def dot_nt(a, b):
    return lax.dot_general(a, b, (((1,), (1,)), ((), ())), preferred_element_type=F32)


def kernel(
    bias_ref, win_ref, cnt_ref, q_hbm, k_hbm, v_hbm, a_hbm, h_hbm, dw_hbm, uw_hbm,
    fin_u_out, fin_d_out, bias_out,
    kv, sink, bb, wu, wd, q_s, a_s, h_s, o_s, t_s, kt, ve, mask, score_a, score_b,
    gu, gd, rcu, rcd, rau, rad, s2u, s2d, rbu, rbd, s3u, s3d, r3u, r3d, finu, find,
    bg, bgz, bgs, bgx, bgf,
    ld, kv_s, kv_r, sk, bb_s, bb_r, w_s, w_r, rs_s, rs_r, bg_s, bg_r,
):
    dp, ctx = lax.axis_index("dp"), lax.axis_index("ctx")
    y, c, x, z = dp // 2, dp % 2, ctx // NZ, ctx % NZ

    def dev(x_=x, y_=y, z_=z, c_=c):
        return (y_ * 2 + c_, x_ * NZ + z_)

    def off(v, i, n):
        return lax.rem(v + i + n, n)

    right, left = (dp, off(ctx, 1, N_CTX)), (dp, off(ctx, -1, N_CTX))
    jump = (dp, off(ctx, NZ, N_CTX))
    sibling = dev(c_=1 - c)

    def rcopy(src, dst, send, recv, device):
        return pltpu.make_async_remote_copy(
            src_ref=src, dst_ref=dst, send_sem=send, recv_sem=recv, device_id=device, device_id_type=MESH
        )

    def push(src, dst, send, recv, device):
        rcopy(src, dst, send, recv, device).start()

    def arrived(ref, recv):
        rcopy(ref, ref, recv, recv, right).wait_recv()

    def left_here(ref, send):
        rcopy(ref, ref, send, send, right).wait_send()

    for g in range(KV_HEADS):
        cols = pl.ds(g * HEAD_DIM, HEAD_DIM)
        pltpu.make_async_copy(k_hbm.at[0, :, cols], kv.at[0, g, :, pl.ds(0, HEAD_DIM)], ld.at[0]).start()
        pltpu.make_async_copy(v_hbm.at[0, :, cols], kv.at[0, g, :, pl.ds(HEAD_DIM, HEAD_DIM)], ld.at[0]).start()
    for half in range(2):
        rows = pl.multiple_of(dp % 4 * 2 * DOWN_ROWS + half * DOWN_ROWS, DOWN_ROWS)
        cols = pl.multiple_of(dp // 4 * HEAD_DIM, HEAD_DIM)
        pltpu.make_async_copy(
            dw_hbm.at[pl.ds(rows, DOWN_ROWS), pl.ds(cols, HEAD_DIM)], wd.at[half, c, x, y, z], ld.at[1]
        ).start()
        rows = pl.multiple_of(dp * 2 * UP_ROWS + half * UP_ROWS, UP_ROWS)
        pltpu.make_async_copy(uw_hbm.at[pl.ds(rows, UP_ROWS), :], wu.at[half, c, x, y, z], ld.at[2]).start()
    late = [
        pltpu.make_async_copy(q_hbm.at[0], q_s, ld.at[3]),
        pltpu.make_async_copy(a_hbm.at[0], a_s, ld.at[4]),
        pltpu.make_async_copy(h_hbm.at[0], h_s, ld.at[5]),
    ]
    for copy in late:
        copy.start()

    barrier = pltpu.get_barrier_semaphore()
    partners = [left, right]
    partners += [dev(x_=off(x, i, NX)) for i in range(1, NX)]
    partners += [dev(z_=off(z, i, NZ)) for i in range(1, NZ)]
    partners += [(off(dp, i, N_DP), ctx) for i in range(1, N_DP)]
    for partner in partners:
        pl.semaphore_signal(barrier, inc=1, device_id=partner, device_id_type=MESH)
    row8 = lax.broadcasted_iota(jnp.int32, (8, HEAD_DIM), 0)
    bb[x, z] = jnp.where(row8 == 1, bias_ref[1], bias_ref[0]) * LOG2E
    for n, ref in enumerate((kv.at[0], wd.at[:, c, x, y, z], wu.at[:, c, x, y, z])):
        pltpu.make_async_copy(ref, ref, ld.at[n]).wait()

    @pl.when(ctx == 0)
    def _():
        for g in range(KV_HEADS):
            sink[g] = kv[0, g, 0:SINKS, :]

    pl.semaphore_wait(barrier, len(partners))

    first_z = z == 0
    far_slot = jnp.where(first_z, 7, 8)
    far_device = (dp, jnp.where(first_z, x * NZ + NZ - 1, off(ctx, NZ, N_CTX)))

    def kv_push(g, src, dst, device):
        push(kv.at[src, g], kv.at[dst, g], kv_s.at[0], kv_r.at[dst, g], device)

    def kv_arrived(g, slot):
        arrived(kv.at[slot, g], kv_r.at[slot, g])

    def kv_hop(g, step):
        kv_arrived(g, step)
        kv_push(g, step, step + 1, right)
        if step == 1:

            @pl.when(z != 0)
            def _():
                kv_arrived(g, 8)
                kv_push(g, 8, 7, left)

        else:
            kv_arrived(g, 9 - step)
            kv_push(g, 9 - step, 8 - step, left)

    def sink_copies(axis):
        if axis == "x":
            return [rcopy(sink, sink, sk.at[0], sk.at[2], dev(x_=off(x, i, NX))) for i in range(1, NX)]
        return [rcopy(sink, sink, sk.at[1], sk.at[2], dev(z_=off(z, i, NZ))) for i in range(1, NZ)]

    @pl.when(ctx == 0)
    def _():
        for copy in sink_copies("x"):
            copy.start()

    weights = (wd, wu)
    Z_STAGE, SECOND_STAGE, Y_BELOW, Y_ABOVE, Y_ONWARD, X_BELOW, X_ABOVE, X_ONWARD, SIBLING = range(9)
    above, below = off(y, 1, NY), off(y, -1, NY)
    x_above, x_below = off(x, 1, NX), off(x, -1, NX)
    low, high = pl.ds(0, 2), pl.ds(2, 2)

    def w_push(part, stage, src, device):
        push(src, src, w_s.at[part, stage], w_r.at[part, stage], device)

    w_sizes = (
        {
            Z_STAGE: wd.at[0, c, 0, low, pl.ds(0, 7)], SECOND_STAGE: wd.at[0, c, pl.ds(0, 3), low],
            Y_BELOW: wd.at[:, c, 0], Y_ABOVE: wd.at[:, c, 0], Y_ONWARD: wd.at[:, c, 0], SIBLING: wd.at[:, c],
        },
        {
            Z_STAGE: wu.at[0, c, 0, low, pl.ds(0, 7)], SECOND_STAGE: wu.at[0, c, pl.ds(0, 3), low],
            Y_BELOW: wu.at[0, c, 0], Y_ABOVE: wu.at[0, c, 0], Y_ONWARD: wu.at[0, c, 0],
            X_BELOW: wu.at[0, c, 0], X_ABOVE: wu.at[0, c, 0], X_ONWARD: wu.at[0, c, 0], SIBLING: wu.at[:, c],
        },
    )

    def w_arrived(part, stage):
        arrived(w_sizes[part][stage], w_r.at[part, stage])

    def along_z(part):
        for i in range(1, NZ):
            w_push(part, Z_STAGE, weights[part].at[:, c, x, y, z], dev(z_=off(z, i, NZ)))

    def second(part):
        w = weights[part]
        w_arrived(part, Z_STAGE)
        for i in range(1, NX):
            if part == 0:
                w_push(part, SECOND_STAGE, w.at[:, c, x, y], dev(x_=off(x, i, NX)))
            else:
                w_push(part, SECOND_STAGE, w.at[0, c, x, y], dev(x_=off(x, i, NX)))
                w_push(part, SECOND_STAGE, w.at[1, c, x, y], dev(y_=off(y, i, NY)))

    def rings(part):
        w = weights[part]
        w_arrived(part, SECOND_STAGE)
        for half in range(2):
            if part == 1 and half == 1:
                w_push(part, X_BELOW, w.at[1, c, x], dev(x_=x_above))
                w_push(part, X_ABOVE, w.at[1, c, x], dev(x_=x_below))
            else:
                w_push(part, Y_BELOW, w.at[half, c, :, y], dev(y_=above))
                w_push(part, Y_ABOVE, w.at[half, c, :, y], dev(y_=below))

    def y_onward(part):
        w_arrived(part, Y_BELOW)
        from_below = wd.at[0, c, :, below] if part == 0 else wu.at[0, c, low, below]
        w_push(part, Y_ONWARD, from_below, dev(y_=above))
        w_arrived(part, Y_ABOVE)
        from_above = wd.at[1, c, :, above] if part == 0 else wu.at[0, c, high, above]
        w_push(part, Y_ONWARD, from_above, dev(y_=below))

    def x_onward(part):
        w_arrived(part, X_BELOW)
        w_push(part, X_ONWARD, wu.at[1, c, x_below, low], dev(x_=x_above))
        w_arrived(part, X_ABOVE)
        w_push(part, X_ONWARD, wu.at[1, c, x_above, high], dev(x_=x_below))

    def to_sibling(part):
        w_arrived(part, Y_ONWARD)
        if part == 1:
            w_arrived(part, X_ONWARD)
        w_push(part, SIBLING, weights[part].at[:, c], sibling)

    def spread_jump(g):
        @pl.when(first_z)
        def _():
            kv_push(g, 0, 8, jump)

    along_z(0)
    for g in range(KV_HEADS):
        kv_push(g, 0, 1, right)
        kv_push(g, 0, far_slot, far_device)
    spread_jump(0)
    for i in range(1, NZ):
        push(bb.at[x, z], bb.at[x, z], bb_s.at[0], bb_r.at[0], dev(z_=off(z, i, NZ)))
    along_z(1)

    window, count = win_ref[0], cnt_ref[0]
    row = lax.broadcasted_iota(jnp.int32, (TOK, TOK), 0)
    col = lax.broadcasted_iota(jnp.int32, (TOK, TOK), 1)
    causal = col <= row

    def seen(block):
        return (block * TOK + row - col < window) & ((ctx - block) * TOK + col >= count)

    for j in range(7):
        mask[:, j * TOK : (j + 1) * TOK] = jnp.where(seen(ORDER[j]), 0.0, MASKED)
    both = jnp.where(causal, jnp.where(seen(0), 1, 0), jnp.where(seen(8), 1, 0)) == 1
    mask[:, 7 * TOK : 8 * TOK] = jnp.where(both, 0.0, MASKED)
    sink_seen = (col <= ctx * TOK + row) & (col < count)
    mask[:, 8 * TOK :] = jnp.where(sink_seen, 0.0, MASKED)
    ve[:, HEAD_DIM:] = jnp.ones((COLS, HEAD_DIM), BF16)
    ve[BLOCKS * TOK :, 0:HEAD_DIM] = jnp.zeros((TOK, HEAD_DIM), BF16)
    bg[...] = jnp.zeros(bg.shape, F32)

    second(0)
    for g in range(KV_HEADS):
        kv_hop(g, 1)
    spread_jump(1)

    @pl.when((z == 0) & (x != 0))
    def _():
        arrived(sink, sk.at[2])

    @pl.when(z == 0)
    def _():
        for copy in sink_copies("z"):
            copy.start()

    arrived(bb.at[0, pl.ds(0, 7)], bb_r.at[0])
    for i in range(1, NX):
        push(bb.at[x], bb.at[x], bb_s.at[1], bb_r.at[1], dev(x_=off(x, i, NX)))
    second(1)
    rings(0)

    for g in range(KV_HEADS):
        kv_hop(g, 2)
    spread_jump(2)
    rings(1)

    arrived(bb.at[pl.ds(0, 3)], bb_r.at[1])

    @pl.when(z != 0)
    def _():
        arrived(sink, sk.at[2])

    for g in range(KV_HEADS):
        kv_hop(g, 3)
    spread_jump(3)
    y_onward(0)
    late[0].wait()

    def columns(head):
        return pl.ds(pl.multiple_of(head * HEAD_DIM, HEAD_DIM), HEAD_DIM)

    rows = HEAD_STEP * TOK

    def score_heads(first, score_s):
        queries = jnp.concatenate([q_s[:, columns(first + e)] for e in range(HEAD_STEP)], axis=0)
        score = (dot(queries, kt[...]) * SCORE_SCALE).reshape(HEAD_STEP, TOK, COLS)

        def tile(j):
            return score[:, :, j * TOK : (j + 1) * TOK]

        biases = []
        for e in range(HEAD_STEP):
            shard = (first + e) // 2
            biases.append(bb[shard // NZ, shard % NZ, e % 2 : e % 2 + 1, :][None])
        top = None
        for j in range(BLOCKS):
            seen_j = mask[:, j * TOK : (j + 1) * TOK][None]
            if j < 7:
                part = tile(j) + seen_j
            elif j == 7:
                part = jnp.where(causal[None], tile(7), tile(8)) + seen_j
            else:
                part = tile(9) + (seen_j + jnp.concatenate(biases, axis=0))
            score_s[:, :, j * TOK : (j + 1) * TOK] = part
            top = part if top is None else jnp.maximum(top, part)
        return jnp.max(top, axis=-1, keepdims=True)

    def finish_heads(first, score_s, top):
        probs = [jnp.exp2(score_s[:, :, j * TOK : (j + 1) * TOK] - top).astype(BF16) for j in range(BLOCKS)]
        nothing = jnp.zeros((), BF16)
        near = jnp.where(causal[None], probs[7], nothing)
        far = jnp.where(causal[None], nothing, probs[7])
        local = jnp.concatenate(probs[:7] + [near, far], axis=-1).reshape(rows, BLOCKS * TOK)
        from_sinks = dot(probs[8].reshape(rows, TOK), ve[BLOCKS * TOK :, :])
        total = dot(local, ve[0 : BLOCKS * TOK, :]) + from_sinks
        scale = 1.0 / total[:, HEAD_DIM:]
        out = (total[:, 0:HEAD_DIM] * scale).astype(BF16)
        term = (from_sinks[:, 0:HEAD_DIM] - from_sinks[:, HEAD_DIM:] * out.astype(F32)) * scale
        for e in range(HEAD_STEP):
            o_s[:, columns(first + e)] = out[e * TOK : (e + 1) * TOK]
            t_s[:, columns(first + e)] = term[e * TOK : (e + 1) * TOK]

    def attend_heads(first):
        steps = GROUP // HEAD_STEP
        held = (score_a, score_b)
        top = score_heads(first, held[0])
        for n in range(steps):
            later = score_heads(first + (n + 1) * HEAD_STEP, held[(n + 1) % 2]) if n + 1 < steps else None
            finish_heads(first + n * HEAD_STEP, held[n % 2], top)
            top = later

    def attend_group(g, carry):
        kv_arrived(g, 4)
        kv_arrived(g, 5)

        @pl.when(first_z)
        def _():
            kv_arrived(g, 8)

        for j, block in enumerate(ORDER):
            kt[:, j * TOK : (j + 1) * TOK] = kv[block, g, :, 0:HEAD_DIM].T
            ve[j * TOK : (j + 1) * TOK, 0:HEAD_DIM] = kv[block, g, :, HEAD_DIM:]
        padded = jnp.concatenate([sink[g, :, 0:HEAD_DIM], jnp.zeros((TOK - SINKS, HEAD_DIM), BF16)], axis=0)
        kt[:, BLOCKS * TOK :] = padded.T
        ve[BLOCKS * TOK : BLOCKS * TOK + SINKS, 0:HEAD_DIM] = sink[g, :, HEAD_DIM:]
        attend_heads(g * GROUP)

        @pl.when(g == 0)
        def _():
            y_onward(1)
            x_onward(1)

        @pl.when(g == 1)
        def _():
            to_sibling(0)

        @pl.when(g == 2)
        def _():
            to_sibling(1)

        return carry

    lax.fori_loop(0, KV_HEADS, attend_group, 0)

    pieces = [(half, p % 2, p // 2) for p in range(N_DP) for half in range(2)]

    def down_weight(xs, zs):
        return [
            jnp.concatenate([wd[half, cs, xs, ys, zs] for half, cs, ys in pieces[8 * e : 8 * e + 8]], axis=0)
            for e in range(2)
        ]

    w_arrived(0, SIBLING)

    def low_out_step(xs, total):
        down = jnp.concatenate([w for zs in range(NZ) for w in down_weight(xs, zs)], axis=1)
        return total + dot_nt(down, o_s[:, pl.ds(pl.multiple_of(xs * 2048, 2048), 2048)])

    low_out_t = lax.fori_loop(0, NX, low_out_step, jnp.zeros((RANK, TOK), F32)).astype(BF16)
    late[1].wait()

    grads, from_core = (gd, gu), (rcd, rcu)
    first_in, first_sum = (rad, rau), (s2d, s2u)
    second_in, second_sum = (rbd, rbu), (s3d, s3u)
    third_in, final = (r3d, r3u), (find, finu)
    order = [off(x, i, NX) for i in (1, 2, 3, 0)]

    CORE, FIRST, SECOND, THIRD, LAST = 0, 4, 5, 6, 7
    rs_sizes = [
        {CORE: from_core[p], FIRST: first_in[p], SECOND: second_in[p], THIRD: third_in[p], LAST: final[p].at[pl.ds(0, 7)]}
        for p in range(2)
    ]

    def rs_push(part, stage, src, dst, device, row=0):
        push(src, dst, rs_s.at[part, stage], rs_r.at[part, stage + row], device)

    def rs_arrived(part, stage):
        arrived(rs_sizes[part][stage], rs_r.at[part, stage])

    def to_core(part, j):
        xs = order[j]
        rs_push(part, CORE, grads[part].at[:, 1 - c, xs], from_core[part].at[:, xs], sibling, j)

    def first_stage(part, j):
        xs = order[j]
        arrived(from_core[part].at[:, xs], rs_r.at[part, j])
        mine, theirs = grads[part], from_core[part]

        def one(n, carry):
            half, ys = n // NY, n % NY
            mine[half, c, xs, ys] = (mine[half, c, xs, ys].astype(F32) + theirs[half, xs, ys].astype(F32)).astype(BF16)
            return carry

        lax.fori_loop(0, 2 * NY, one, 0)
        for i in range(1, NY):
            rs_push(part, FIRST, mine.at[0, c, xs, off(y, i, NY)], first_in[part].at[0, i - 1, xs], dev(y_=off(y, i, NY)))
        if j < 3:
            rs_push(part, FIRST, mine.at[1, c, xs], first_in[part].at[1, j], dev(x_=xs))

    def second_stage(part):
        rs_arrived(part, FIRST)
        mine, theirs, total = grads[part], first_in[part], first_sum[part]

        def one(n, carry):
            for half, own in ((0, mine.at[0, c, n, y]), (1, mine.at[1, c, x, n])):
                acc = own[...].astype(F32)
                for i in range(3):
                    acc = acc + theirs[half, i, n].astype(F32)
                total[half, n] = acc.astype(BF16)
            return carry

        lax.fori_loop(0, 4, one, 0)
        for i in range(1, NX):
            to_x, to_y = off(x, i, NX), off(y, i, NY)
            rs_push(part, SECOND, total.at[0, to_x], second_in[part].at[0, i - 1], dev(x_=to_x))
            rs_push(part, SECOND, total.at[1, to_y], second_in[part].at[1, i - 1], dev(y_=to_y))

    def third_stage(part):
        rs_arrived(part, SECOND)
        mine, theirs, total = first_sum[part], second_in[part], second_sum[part]
        for half, own in ((0, x), (1, y)):
            acc = mine[half, own].astype(F32)
            for i in range(3):
                acc = acc + theirs[half, i].astype(F32)
            total[:, half] = acc.astype(BF16)
        for i in range(1, NZ):
            rs_push(part, THIRD, total.at[off(z, i, NZ)], third_in[part].at[i - 1], dev(z_=off(z, i, NZ)))

    def last_stage(part):
        rs_arrived(part, THIRD)
        acc = second_sum[part][z].astype(F32)
        for i in range(1, NZ):
            acc = acc + third_in[part][i - 1].astype(F32)
        final[part][dp] = acc.astype(BF16)
        for i in range(1, N_DP):
            rs_push(part, LAST, final[part].at[dp], final[part].at[dp], (off(dp, i, N_DP), ctx))

    def last_arrived(part):
        rs_arrived(part, LAST)

    def up_row(xs):
        def step(zs, carry):
            cols = pl.ds(pl.multiple_of((xs * NZ + zs) * 512, 512), 512)
            grad = (2.0 * dot(low_out_t, a_s[:, cols])).astype(BF16)
            for p in range(N_DP):
                for half in range(2):
                    for j in range(2):
                        lane = 256 * half + 128 * j
                        gu[half, p % 2, xs, p // 2, zs, 16 * j : 16 * j + 16, :] = grad[
                            16 * p : 16 * p + 16, lane : lane + 128
                        ]
            return carry

        lax.fori_loop(0, NZ, step, 0, unroll=2)

    for j in range(NX):
        up_row(order[j])
        to_core(1, j)
        if j > 0:
            first_stage(1, j - 1)
    first_stage(1, 3)

    w_arrived(1, SIBLING)

    def low_grad_step(xs, total):
        up = jnp.concatenate(
            [wu[half, cs, xs, ys, zs] for zs in range(NZ) for half, cs, ys in pieces], axis=0
        )
        return total + dot(a_s[:, pl.ds(pl.multiple_of(xs * 4096, 4096), 4096)], up)

    low_grad = lax.fori_loop(0, NX, low_grad_step, jnp.zeros((TOK, RANK), F32))
    low_grad_t = low_grad.T.astype(BF16)
    low_grad = low_grad.astype(BF16)
    late[2].wait()

    def down_row(xs):
        def step(zs, carry):
            cols = pl.ds(pl.multiple_of((xs * NZ + zs) * 256, 256), 256)
            down = jnp.concatenate(down_weight(xs, zs), axis=1)
            head_total = (h_s[:, cols].astype(F32) + 2.0 * dot(low_grad, down)).astype(BF16)
            bias_terms = jnp.sum(head_total.astype(F32) * t_s[:, cols], axis=0, keepdims=True)
            for e in range(2):
                bg[zs, xs, e : e + 1, :] = bias_terms[:, e * HEAD_DIM : (e + 1) * HEAD_DIM]
            grad = (2.0 * dot(low_grad_t, o_s[:, cols])).astype(BF16)
            for n, (half, cs, ys) in enumerate(pieces):
                e, r = n // 8, n % 8 * DOWN_ROWS
                gd[half, cs, xs, ys, zs] = grad[r : r + DOWN_ROWS, e * HEAD_DIM : (e + 1) * HEAD_DIM]
            return carry

        lax.fori_loop(0, NZ, step, 0, unroll=2)

    for j in range(NX):
        down_row(order[j])
        to_core(0, j)
        if j > 0:
            first_stage(0, j - 1)

    for i in range(1, NZ):
        push(bg.at[off(z, i, NZ)], bgz.at[i - 1], bg_s.at[0], bg_r.at[0], dev(z_=off(z, i, NZ)))
    first_stage(0, 3)
    second_stage(1)

    arrived(bgz, bg_r.at[0])
    terms = bg[z]
    for i in range(1, NZ):
        terms = terms + bgz[i - 1]
    bgs[...] = terms
    for i in range(1, NX):
        push(bgs.at[off(x, i, NX)], bgx.at[i - 1], bg_s.at[1], bg_r.at[1], dev(x_=off(x, i, NX)))

    second_stage(0)
    third_stage(1)

    arrived(bgx, bg_r.at[1])
    terms = bgs[x]
    for i in range(1, NX):
        terms = terms + bgx[i - 1]
    bgf[dp] = terms
    for i in range(1, N_DP):
        push(bgf.at[dp], bgf.at[dp], bg_s.at[2], bg_r.at[2], (off(dp, i, N_DP), ctx))

    third_stage(0)
    last_stage(1)
    last_stage(0)

    arrived(bgf.at[pl.ds(0, 7)], bg_r.at[2])
    terms = bgf[0]
    for p in range(1, N_DP):
        terms = terms + bgf[p]
    bias_out[...] = terms
    last_arrived(1)
    fin_u_out[...] = finu[...]
    last_arrived(0)
    fin_d_out[...] = find[...]

    left_here(kv.at[pl.ds(1, 8)], kv_s.at[0])
    left_here(bb.at[0, pl.ds(0, 7)], bb_s.at[0])
    left_here(bb.at[pl.ds(0, 3)], bb_s.at[1])
    for part in range(2):
        for stage, ref in w_sizes[part].items():
            left_here(ref, w_s.at[part, stage])
        for stage, ref in rs_sizes[part].items():
            left_here(ref, rs_s.at[part, stage])
    left_here(bgz, bg_s.at[0])
    left_here(bgx, bg_s.at[1])
    left_here(bgf.at[pl.ds(0, 7)], bg_s.at[2])

    @pl.when(ctx == 0)
    def _():
        left_here(kv.at[0, :, pl.ds(0, 3 * SINKS), :], sk.at[0])

    @pl.when(z == 0)
    def _():
        left_here(kv.at[0, :, pl.ds(0, 7 * SINKS), :], sk.at[1])


def write_out(fin_u, fin_d, terms, down_out, up_out, bias_out):
    for b in range(4):
        block = jnp.concatenate([fin_u[p, b // 2, 16 * (b % 2) : 16 * (b % 2) + 16, :] for p in range(N_DP)], axis=0)
        up_out[128 * b : 128 * b + 128, :] = block.astype(F32).T
    for e in range(2):
        block = jnp.concatenate([fin_d[4 * e + n // 2, n % 2] for n in range(8)], axis=0)
        down_out[:, e * HEAD_DIM : (e + 1) * HEAD_DIM] = block.astype(F32)
    bias_out[0] = jnp.sum(terms[0:1, :])
    bias_out[1] = jnp.sum(terms[1:2, :])


def on_device(q, k, v, a, h, bias, windows, counts, down, up):
    hbm, smem, vmem = (pl.BlockSpec(memory_space=s) for s in (pl.ANY, pltpu.SMEM, pltpu.VMEM))
    sem = pltpu.SemaphoreType.DMA
    heads = HEADS * HEAD_DIM

    def pair(*dims):
        return [pltpu.VMEM(dims + (rows, HEAD_DIM), BF16) for rows in (UP_ROWS, DOWN_ROWS)]

    scratch = [
        pltpu.VMEM((BLOCKS, KV_HEADS, TOK, 2 * HEAD_DIM), BF16),
        pltpu.VMEM((KV_HEADS, SINKS, 2 * HEAD_DIM), BF16),
        pltpu.VMEM((NX, NZ, 8, HEAD_DIM), F32),
        *pair(2, 2, NX, NY, NZ),
        pltpu.VMEM((TOK, heads), BF16),
        pltpu.VMEM((TOK, a.shape[2]), BF16),
        pltpu.VMEM((TOK, heads), BF16),
        pltpu.VMEM((TOK, heads), BF16),
        pltpu.VMEM((TOK, heads), F32),
        pltpu.VMEM((HEAD_DIM, COLS), BF16),
        pltpu.VMEM((COLS, 2 * HEAD_DIM), BF16),
        pltpu.VMEM((TOK, BLOCKS * TOK), F32),
        pltpu.VMEM((HEAD_STEP, TOK, BLOCKS * TOK), F32),
        pltpu.VMEM((HEAD_STEP, TOK, BLOCKS * TOK), F32),
        *pair(2, 2, NX, NY, NZ),
        *pair(2, NX, NY, NZ),
        *pair(2, 3, 4, NZ),
        *pair(2, 4, NZ),
        *pair(2, 3, NZ),
        *pair(NZ, 2),
        *pair(NZ - 1, 2),
        *pair(N_DP, 2),
        pltpu.VMEM((NZ, NX, 8, HEAD_DIM), F32),
        pltpu.VMEM((NZ - 1, NX, 8, HEAD_DIM), F32),
        pltpu.VMEM((NX, 8, HEAD_DIM), F32),
        pltpu.VMEM((NX - 1, 8, HEAD_DIM), F32),
        pltpu.VMEM((N_DP, 8, HEAD_DIM), F32),
        sem((6,)),
        sem((1,)),
        sem((BLOCKS, KV_HEADS)),
        sem((3,)),
        sem((2,)),
        sem((2,)),
        sem((2, 9)),
        sem((2, 9)),
        sem((2, 8)),
        sem((2, 8)),
        sem((3,)),
        sem((3,)),
    ]
    reduced = pl.pallas_call(
        kernel,
        out_shape=(
            jax.ShapeDtypeStruct((N_DP, 2, UP_ROWS, HEAD_DIM), BF16),
            jax.ShapeDtypeStruct((N_DP, 2, DOWN_ROWS, HEAD_DIM), BF16),
            jax.ShapeDtypeStruct((8, HEAD_DIM), F32),
        ),
        in_specs=[smem] * 3 + [hbm] * 7,
        out_specs=(vmem, vmem, vmem),
        scratch_shapes=scratch,
        compiler_params=pltpu.CompilerParams(
            collective_id=0, has_side_effects=True, vmem_limit_bytes=60 * 1024 * 1024
        ),
        name="token_parallel",
    )(bias, windows, counts, q, k, v, a, h, down, up)
    return pl.pallas_call(
        write_out,
        out_shape=(
            jax.ShapeDtypeStruct(down.shape, F32),
            jax.ShapeDtypeStruct(up.shape, F32),
            jax.ShapeDtypeStruct(bias.shape, F32),
        ),
        in_specs=[vmem] * 3,
        out_specs=(vmem, vmem, smem),
        name="write_out",
    )(*reduced)


def solution(mesh):
    rows = P("dp", "ctx", None)
    placed = (rows,) * 5 + (P("ctx"), P("dp"), P("dp"), P(None, "ctx"), P("ctx", None))
    return jax.shard_map(
        on_device,
        mesh=mesh,
        in_specs=placed,
        out_specs=(P(None, "ctx"), P("ctx", None), P("ctx")),
        check_vma=False,
    )
```

```python
import jax
import jax.numpy as jnp
from jax import lax
from jax.experimental import pallas as pl
from jax.experimental.pallas import tpu as pltpu
from jax.sharding import PartitionSpec as P

NX, NY, NZ = 4, 4, 8
N_CTX, N_DP = NX * NZ, NY * 2
TOK = 128
HEAD_DIM = 128
KV_HEADS = 4
GROUP = 16
HEADS = KV_HEADS * GROUP
RANK = 128
SINKS = 16
BLOCKS = 9
RELAY = 9
UP_ROWS, DOWN_ROWS = 32, 16
HEAD_STEP = 4
MASKED = -1e30
LOG2E = 1.4426950408889634
SCORE_SCALE = LOG2E * HEAD_DIM**-0.5
BF16, F32 = jnp.bfloat16, jnp.float32
MESH = pl.DeviceIdType.MESH

ORDER = (1, 2, 3, 4, 5, 6, 7, 0, 8)
COLS = 10 * TOK


def dot(a, b):
    return lax.dot_general(a, b, (((1,), (0,)), ((), ())), preferred_element_type=F32)


def dot_nt(a, b):
    return lax.dot_general(a, b, (((1,), (1,)), ((), ())), preferred_element_type=F32)


def kernel(
    bias_ref, win_ref, cnt_ref, q_hbm, k_hbm, v_hbm, a_hbm, h_hbm, dw_hbm, uw_hbm,
    fin_u_out, fin_d_out, bias_out,
    kv, sink, bb, wu, wd, q_s, a_s, h_s, o_s, t_s, kt, ve, mask, score_a, score_b,
    gu, gd, rcu, rcd, rau, rad, s2u, s2d, rbu, rbd, s3u, s3d, r3u, r3d, finu, find,
    bg, bgz, bgs, bgx, bgf,
    ld, kv_s, kv_r, sk, bb_s, bb_r, w_s, w_r, rs_s, rs_r, bg_s, bg_r,
):
    dp, ctx = lax.axis_index("dp"), lax.axis_index("ctx")
    y, c, x, z = dp // 2, dp % 2, ctx // NZ, ctx % NZ

    def dev(x_=x, y_=y, z_=z, c_=c):
        return (y_ * 2 + c_, x_ * NZ + z_)

    def off(v, i, n):
        return lax.rem(v + i + n, n)

    right, left = (dp, off(ctx, 1, N_CTX)), (dp, off(ctx, -1, N_CTX))
    jump = (dp, off(ctx, NZ, N_CTX))
    sibling = dev(c_=1 - c)

    def rcopy(src, dst, send, recv, device):
        return pltpu.make_async_remote_copy(
            src_ref=src, dst_ref=dst, send_sem=send, recv_sem=recv, device_id=device, device_id_type=MESH
        )

    def push(src, dst, send, recv, device):
        rcopy(src, dst, send, recv, device).start()

    def arrived(ref, recv):
        rcopy(ref, ref, recv, recv, right).wait_recv()

    def left_here(ref, send):
        rcopy(ref, ref, send, send, right).wait_send()

    for g in range(KV_HEADS):
        cols = pl.ds(g * HEAD_DIM, HEAD_DIM)
        pltpu.make_async_copy(k_hbm.at[0, :, cols], kv.at[0, g, :, pl.ds(0, HEAD_DIM)], ld.at[0]).start()
        pltpu.make_async_copy(v_hbm.at[0, :, cols], kv.at[0, g, :, pl.ds(HEAD_DIM, HEAD_DIM)], ld.at[0]).start()
    for half in range(2):
        rows = pl.multiple_of(dp % 4 * 2 * DOWN_ROWS + half * DOWN_ROWS, DOWN_ROWS)
        cols = pl.multiple_of(dp // 4 * HEAD_DIM, HEAD_DIM)
        pltpu.make_async_copy(
            dw_hbm.at[pl.ds(rows, DOWN_ROWS), pl.ds(cols, HEAD_DIM)], wd.at[half, c, x, y, z], ld.at[1]
        ).start()
        rows = pl.multiple_of(dp * 2 * UP_ROWS + half * UP_ROWS, UP_ROWS)
        pltpu.make_async_copy(uw_hbm.at[pl.ds(rows, UP_ROWS), :], wu.at[half, c, x, y, z], ld.at[2]).start()
    late = [
        pltpu.make_async_copy(q_hbm.at[0], q_s, ld.at[3]),
        pltpu.make_async_copy(a_hbm.at[0], a_s, ld.at[4]),
        pltpu.make_async_copy(h_hbm.at[0], h_s, ld.at[5]),
    ]
    for copy in late:
        copy.start()

    barrier = pltpu.get_barrier_semaphore()
    partners = [left, right]
    partners += [dev(x_=off(x, i, NX)) for i in range(1, NX)]
    partners += [dev(z_=off(z, i, NZ)) for i in range(1, NZ)]
    partners += [(off(dp, i, N_DP), ctx) for i in range(1, N_DP)]
    for partner in partners:
        pl.semaphore_signal(barrier, inc=1, device_id=partner, device_id_type=MESH)
    row8 = lax.broadcasted_iota(jnp.int32, (8, HEAD_DIM), 0)
    bb[x, z] = jnp.where(row8 == 1, bias_ref[1], bias_ref[0]) * LOG2E
    for n, ref in enumerate((kv.at[0], wd.at[:, c, x, y, z], wu.at[:, c, x, y, z])):
        pltpu.make_async_copy(ref, ref, ld.at[n]).wait()

    @pl.when(ctx == 0)
    def _():
        for g in range(KV_HEADS):
            sink[g] = kv[0, g, 0:SINKS, :]

    pl.semaphore_wait(barrier, len(partners))

    first_z = z == 0
    far_slot = jnp.where(first_z, 7, 8)
    far_device = (dp, jnp.where(first_z, x * NZ + NZ - 1, off(ctx, NZ, N_CTX)))

    def kv_push(g, src, dst, device):
        push(kv.at[src, g], kv.at[dst, g], kv_s.at[0], kv_r.at[dst, g], device)

    def kv_arrived(g, slot):
        arrived(kv.at[slot, g], kv_r.at[slot, g])

    def kv_hop(g, step):
        kv_arrived(g, step)
        kv_push(g, step, step + 1, right)
        if step == 1:

            @pl.when(z != 0)
            def _():
                kv_arrived(g, 8)
                kv_push(g, 8, 7, left)

        else:
            kv_arrived(g, 9 - step)
            kv_push(g, 9 - step, 8 - step, left)

    def sink_copies(axis):
        if axis == "x":
            return [rcopy(sink, sink, sk.at[0], sk.at[2], dev(x_=off(x, i, NX))) for i in range(1, NX)]
        return [rcopy(sink, sink, sk.at[1], sk.at[2], dev(z_=off(z, i, NZ))) for i in range(1, NZ)]

    @pl.when(ctx == 0)
    def _():
        for copy in sink_copies("x"):
            copy.start()

    weights = (wd, wu)
    Z_STAGE, SECOND_STAGE, Y_BELOW, Y_ABOVE, Y_ONWARD, X_BELOW, X_ABOVE, X_ONWARD, SIBLING = range(9)
    above, below = off(y, 1, NY), off(y, -1, NY)
    x_above, x_below = off(x, 1, NX), off(x, -1, NX)
    low, high = pl.ds(0, 2), pl.ds(2, 2)

    def w_push(part, stage, src, device):
        push(src, src, w_s.at[part, stage], w_r.at[part, stage], device)

    w_sizes = (
        {
            Z_STAGE: wd.at[0, c, 0, low, pl.ds(0, 7)], SECOND_STAGE: wd.at[0, c, pl.ds(0, 3), low],
            Y_BELOW: wd.at[:, c, 0], Y_ABOVE: wd.at[:, c, 0], Y_ONWARD: wd.at[:, c, 0], SIBLING: wd.at[:, c],
        },
        {
            Z_STAGE: wu.at[0, c, 0, low, pl.ds(0, 7)], SECOND_STAGE: wu.at[0, c, pl.ds(0, 3), low],
            Y_BELOW: wu.at[0, c, 0], Y_ABOVE: wu.at[0, c, 0], Y_ONWARD: wu.at[0, c, 0],
            X_BELOW: wu.at[0, c, 0], X_ABOVE: wu.at[0, c, 0], X_ONWARD: wu.at[0, c, 0], SIBLING: wu.at[:, c],
        },
    )

    def w_arrived(part, stage):
        arrived(w_sizes[part][stage], w_r.at[part, stage])

    def along_z(part):
        for i in range(1, NZ):
            w_push(part, Z_STAGE, weights[part].at[:, c, x, y, z], dev(z_=off(z, i, NZ)))

    def second(part):
        w = weights[part]
        w_arrived(part, Z_STAGE)
        for i in range(1, NX):
            if part == 0:
                w_push(part, SECOND_STAGE, w.at[:, c, x, y], dev(x_=off(x, i, NX)))
            else:
                w_push(part, SECOND_STAGE, w.at[0, c, x, y], dev(x_=off(x, i, NX)))
                w_push(part, SECOND_STAGE, w.at[1, c, x, y], dev(y_=off(y, i, NY)))

    def rings(part):
        w = weights[part]
        w_arrived(part, SECOND_STAGE)
        for half in range(2):
            if part == 1 and half == 1:
                w_push(part, X_BELOW, w.at[1, c, x], dev(x_=x_above))
                w_push(part, X_ABOVE, w.at[1, c, x], dev(x_=x_below))
            else:
                w_push(part, Y_BELOW, w.at[half, c, :, y], dev(y_=above))
                w_push(part, Y_ABOVE, w.at[half, c, :, y], dev(y_=below))

    def y_onward(part):
        w_arrived(part, Y_BELOW)
        from_below = wd.at[0, c, :, below] if part == 0 else wu.at[0, c, low, below]
        w_push(part, Y_ONWARD, from_below, dev(y_=above))
        w_arrived(part, Y_ABOVE)
        from_above = wd.at[1, c, :, above] if part == 0 else wu.at[0, c, high, above]
        w_push(part, Y_ONWARD, from_above, dev(y_=below))

    def x_onward(part):
        w_arrived(part, X_BELOW)
        w_push(part, X_ONWARD, wu.at[1, c, x_below, low], dev(x_=x_above))
        w_arrived(part, X_ABOVE)
        w_push(part, X_ONWARD, wu.at[1, c, x_above, high], dev(x_=x_below))

    def to_sibling(part):
        w_arrived(part, Y_ONWARD)
        if part == 1:
            w_arrived(part, X_ONWARD)
        w_push(part, SIBLING, weights[part].at[:, c], sibling)

    along_z(0)
    for g in range(KV_HEADS):
        kv_push(g, 0, 1, right)
        kv_push(g, 0, far_slot, far_device)
    for i in range(1, NZ):
        push(bb.at[x, z], bb.at[x, z], bb_s.at[0], bb_r.at[0], dev(z_=off(z, i, NZ)))
    along_z(1)

    window, count = win_ref[0], cnt_ref[0]
    row = lax.broadcasted_iota(jnp.int32, (TOK, TOK), 0)
    col = lax.broadcasted_iota(jnp.int32, (TOK, TOK), 1)
    causal = col <= row

    def seen(block):
        return (block * TOK + row - col < window) & ((ctx - block) * TOK + col >= count)

    for j in range(7):
        mask[:, j * TOK : (j + 1) * TOK] = jnp.where(seen(ORDER[j]), 0.0, MASKED)
    both = jnp.where(causal, jnp.where(seen(0), 1, 0), jnp.where(seen(8), 1, 0)) == 1
    mask[:, 7 * TOK : 8 * TOK] = jnp.where(both, 0.0, MASKED)
    sink_seen = (col <= ctx * TOK + row) & (col < count)
    mask[:, 8 * TOK :] = jnp.where(sink_seen, 0.0, MASKED)
    ve[:, HEAD_DIM:] = jnp.ones((COLS, HEAD_DIM), BF16)
    ve[BLOCKS * TOK :, 0:HEAD_DIM] = jnp.zeros((TOK, HEAD_DIM), BF16)
    bg[...] = jnp.zeros(bg.shape, F32)

    second(0)
    for g in range(KV_HEADS):
        kv_hop(g, 1)

    @pl.when(z == 1)
    def _():
        for g in range(KV_HEADS):
            kv_push(g, 1, RELAY, jump)


    @pl.when((z == 0) & (x != 0))
    def _():
        arrived(sink, sk.at[2])

    @pl.when(z == 0)
    def _():
        for copy in sink_copies("z"):
            copy.start()

    arrived(bb.at[0, pl.ds(0, 7)], bb_r.at[0])
    for i in range(1, NX):
        push(bb.at[x], bb.at[x], bb_s.at[1], bb_r.at[1], dev(x_=off(x, i, NX)))
    second(1)
    rings(0)

    for g in range(KV_HEADS):
        kv_hop(g, 2)


    arrived(bb.at[pl.ds(0, 3)], bb_r.at[1])

    @pl.when(z != 0)
    def _():
        arrived(sink, sk.at[2])

    for g in range(KV_HEADS):
        kv_hop(g, 3)

    @pl.when(z == 1)
    def _():
        for g in range(KV_HEADS):
            kv_arrived(g, RELAY)
            kv_push(g, RELAY, 8, left)

    rings(1)
    y_onward(0)
    late[0].wait()

    def columns(head):
        return pl.ds(pl.multiple_of(head * HEAD_DIM, HEAD_DIM), HEAD_DIM)

    rows = HEAD_STEP * TOK

    def score_heads(first, score_s):
        queries = jnp.concatenate([q_s[:, columns(first + e)] for e in range(HEAD_STEP)], axis=0)
        score = (dot(queries, kt[...]) * SCORE_SCALE).reshape(HEAD_STEP, TOK, COLS)

        def tile(j):
            return score[:, :, j * TOK : (j + 1) * TOK]

        biases = []
        for e in range(HEAD_STEP):
            shard = (first + e) // 2
            biases.append(bb[shard // NZ, shard % NZ, e % 2 : e % 2 + 1, :][None])
        top = None
        for j in range(BLOCKS):
            seen_j = mask[:, j * TOK : (j + 1) * TOK][None]
            if j < 7:
                part = tile(j) + seen_j
            elif j == 7:
                part = jnp.where(causal[None], tile(7), tile(8)) + seen_j
            else:
                part = tile(9) + (seen_j + jnp.concatenate(biases, axis=0))
            score_s[:, :, j * TOK : (j + 1) * TOK] = part
            top = part if top is None else jnp.maximum(top, part)
        return jnp.max(top, axis=-1, keepdims=True)

    def finish_heads(first, score_s, top):
        probs = [jnp.exp2(score_s[:, :, j * TOK : (j + 1) * TOK] - top).astype(BF16) for j in range(BLOCKS)]
        nothing = jnp.zeros((), BF16)
        near = jnp.where(causal[None], probs[7], nothing)
        far = jnp.where(causal[None], nothing, probs[7])
        local = jnp.concatenate(probs[:7] + [near, far], axis=-1).reshape(rows, BLOCKS * TOK)
        from_sinks = dot(probs[8].reshape(rows, TOK), ve[BLOCKS * TOK :, :])
        total = dot(local, ve[0 : BLOCKS * TOK, :]) + from_sinks
        scale = 1.0 / total[:, HEAD_DIM:]
        out = (total[:, 0:HEAD_DIM] * scale).astype(BF16)
        term = (from_sinks[:, 0:HEAD_DIM] - from_sinks[:, HEAD_DIM:] * out.astype(F32)) * scale
        for e in range(HEAD_STEP):
            o_s[:, columns(first + e)] = out[e * TOK : (e + 1) * TOK]
            t_s[:, columns(first + e)] = term[e * TOK : (e + 1) * TOK]

    def attend_heads(first):
        steps = GROUP // HEAD_STEP
        held = (score_a, score_b)
        top = score_heads(first, held[0])
        for n in range(steps):
            later = score_heads(first + (n + 1) * HEAD_STEP, held[(n + 1) % 2]) if n + 1 < steps else None
            finish_heads(first + n * HEAD_STEP, held[n % 2], top)
            top = later

    def attend_group(g, carry):
        kv_arrived(g, 4)
        kv_arrived(g, 5)

        @pl.when(first_z)
        def _():
            kv_arrived(g, 8)

        for j, block in enumerate(ORDER):
            kt[:, j * TOK : (j + 1) * TOK] = kv[block, g, :, 0:HEAD_DIM].T
            ve[j * TOK : (j + 1) * TOK, 0:HEAD_DIM] = kv[block, g, :, HEAD_DIM:]
        padded = jnp.concatenate([sink[g, :, 0:HEAD_DIM], jnp.zeros((TOK - SINKS, HEAD_DIM), BF16)], axis=0)
        kt[:, BLOCKS * TOK :] = padded.T
        ve[BLOCKS * TOK : BLOCKS * TOK + SINKS, 0:HEAD_DIM] = sink[g, :, HEAD_DIM:]
        attend_heads(g * GROUP)

        @pl.when(g == 0)
        def _():
            y_onward(1)
            x_onward(1)

        @pl.when(g == 1)
        def _():
            to_sibling(0)

        @pl.when(g == 2)
        def _():
            to_sibling(1)

        return carry

    lax.fori_loop(0, KV_HEADS, attend_group, 0)

    pieces = [(half, p % 2, p // 2) for p in range(N_DP) for half in range(2)]

    def down_weight(xs, zs):
        return [
            jnp.concatenate([wd[half, cs, xs, ys, zs] for half, cs, ys in pieces[8 * e : 8 * e + 8]], axis=0)
            for e in range(2)
        ]

    w_arrived(0, SIBLING)

    def low_out_step(xs, total):
        down = jnp.concatenate([w for zs in range(NZ) for w in down_weight(xs, zs)], axis=1)
        return total + dot_nt(down, o_s[:, pl.ds(pl.multiple_of(xs * 2048, 2048), 2048)])

    low_out_t = lax.fori_loop(0, NX, low_out_step, jnp.zeros((RANK, TOK), F32)).astype(BF16)
    late[1].wait()

    grads, from_core = (gd, gu), (rcd, rcu)
    first_in, first_sum = (rad, rau), (s2d, s2u)
    second_in, second_sum = (rbd, rbu), (s3d, s3u)
    third_in, final = (r3d, r3u), (find, finu)
    order = [off(x, i, NX) for i in (1, 2, 3, 0)]

    CORE, FIRST, SECOND, THIRD, LAST = 0, 4, 5, 6, 7
    rs_sizes = [
        {CORE: from_core[p], FIRST: first_in[p], SECOND: second_in[p], THIRD: third_in[p], LAST: final[p].at[pl.ds(0, 7)]}
        for p in range(2)
    ]

    def rs_push(part, stage, src, dst, device, row=0):
        push(src, dst, rs_s.at[part, stage], rs_r.at[part, stage + row], device)

    def rs_arrived(part, stage):
        arrived(rs_sizes[part][stage], rs_r.at[part, stage])

    def to_core(part, j):
        xs = order[j]
        rs_push(part, CORE, grads[part].at[:, 1 - c, xs], from_core[part].at[:, xs], sibling, j)

    def first_stage(part, j):
        xs = order[j]
        arrived(from_core[part].at[:, xs], rs_r.at[part, j])
        mine, theirs = grads[part], from_core[part]

        def one(n, carry):
            half, ys = n // NY, n % NY
            mine[half, c, xs, ys] = (mine[half, c, xs, ys].astype(F32) + theirs[half, xs, ys].astype(F32)).astype(BF16)
            return carry

        lax.fori_loop(0, 2 * NY, one, 0)
        for i in range(1, NY):
            rs_push(part, FIRST, mine.at[0, c, xs, off(y, i, NY)], first_in[part].at[0, i - 1, xs], dev(y_=off(y, i, NY)))
        if j < 3:
            rs_push(part, FIRST, mine.at[1, c, xs], first_in[part].at[1, j], dev(x_=xs))

    def second_stage(part):
        rs_arrived(part, FIRST)
        mine, theirs, total = grads[part], first_in[part], first_sum[part]

        def one(n, carry):
            for half, own in ((0, mine.at[0, c, n, y]), (1, mine.at[1, c, x, n])):
                acc = own[...].astype(F32)
                for i in range(3):
                    acc = acc + theirs[half, i, n].astype(F32)
                total[half, n] = acc.astype(BF16)
            return carry

        lax.fori_loop(0, 4, one, 0)
        for i in range(1, NX):
            to_x, to_y = off(x, i, NX), off(y, i, NY)
            rs_push(part, SECOND, total.at[0, to_x], second_in[part].at[0, i - 1], dev(x_=to_x))
            rs_push(part, SECOND, total.at[1, to_y], second_in[part].at[1, i - 1], dev(y_=to_y))

    def third_stage(part):
        rs_arrived(part, SECOND)
        mine, theirs, total = first_sum[part], second_in[part], second_sum[part]
        for half, own in ((0, x), (1, y)):
            acc = mine[half, own].astype(F32)
            for i in range(3):
                acc = acc + theirs[half, i].astype(F32)
            total[:, half] = acc.astype(BF16)
        for i in range(1, NZ):
            rs_push(part, THIRD, total.at[off(z, i, NZ)], third_in[part].at[i - 1], dev(z_=off(z, i, NZ)))

    def last_stage(part):
        rs_arrived(part, THIRD)
        acc = second_sum[part][z].astype(F32)
        for i in range(1, NZ):
            acc = acc + third_in[part][i - 1].astype(F32)
        final[part][dp] = acc.astype(BF16)
        for i in range(1, N_DP):
            rs_push(part, LAST, final[part].at[dp], final[part].at[dp], (off(dp, i, N_DP), ctx))

    def last_arrived(part):
        rs_arrived(part, LAST)

    def up_row(xs):
        def step(zs, carry):
            cols = pl.ds(pl.multiple_of((xs * NZ + zs) * 512, 512), 512)
            grad = (2.0 * dot(low_out_t, a_s[:, cols])).astype(BF16)
            for p in range(N_DP):
                for half in range(2):
                    for j in range(2):
                        lane = 256 * half + 128 * j
                        gu[half, p % 2, xs, p // 2, zs, 16 * j : 16 * j + 16, :] = grad[
                            16 * p : 16 * p + 16, lane : lane + 128
                        ]
            return carry

        lax.fori_loop(0, NZ, step, 0, unroll=4)

    for j in range(NX):
        up_row(order[j])
        to_core(1, j)
        if j > 0:
            first_stage(1, j - 1)
    first_stage(1, 3)

    w_arrived(1, SIBLING)

    def low_grad_step(xs, total):
        up = jnp.concatenate(
            [wu[half, cs, xs, ys, zs] for zs in range(NZ) for half, cs, ys in pieces], axis=0
        )
        return total + dot(a_s[:, pl.ds(pl.multiple_of(xs * 4096, 4096), 4096)], up)

    low_grad = lax.fori_loop(0, NX, low_grad_step, jnp.zeros((TOK, RANK), F32))
    low_grad_t = low_grad.T.astype(BF16)
    low_grad = low_grad.astype(BF16)
    late[2].wait()

    def down_row(xs):
        def step(zs, carry):
            cols = pl.ds(pl.multiple_of((xs * NZ + zs) * 256, 256), 256)
            down = jnp.concatenate(down_weight(xs, zs), axis=1)
            head_total = (h_s[:, cols].astype(F32) + 2.0 * dot(low_grad, down)).astype(BF16)
            bias_terms = jnp.sum(head_total.astype(F32) * t_s[:, cols], axis=0, keepdims=True)
            for e in range(2):
                bg[zs, xs, e : e + 1, :] = bias_terms[:, e * HEAD_DIM : (e + 1) * HEAD_DIM]
            grad = (2.0 * dot(low_grad_t, o_s[:, cols])).astype(BF16)
            for n, (half, cs, ys) in enumerate(pieces):
                e, r = n // 8, n % 8 * DOWN_ROWS
                gd[half, cs, xs, ys, zs] = grad[r : r + DOWN_ROWS, e * HEAD_DIM : (e + 1) * HEAD_DIM]
            return carry

        lax.fori_loop(0, NZ, step, 0, unroll=4)

    for j in range(NX):
        down_row(order[j])
        to_core(0, j)
        if j > 0:
            first_stage(0, j - 1)

    for i in range(1, NZ):
        push(bg.at[off(z, i, NZ)], bgz.at[i - 1], bg_s.at[0], bg_r.at[0], dev(z_=off(z, i, NZ)))
    first_stage(0, 3)
    second_stage(1)

    arrived(bgz, bg_r.at[0])
    terms = bg[z]
    for i in range(1, NZ):
        terms = terms + bgz[i - 1]
    bgs[...] = terms
    for i in range(1, NX):
        push(bgs.at[off(x, i, NX)], bgx.at[i - 1], bg_s.at[1], bg_r.at[1], dev(x_=off(x, i, NX)))

    second_stage(0)
    third_stage(1)

    arrived(bgx, bg_r.at[1])
    terms = bgs[x]
    for i in range(1, NX):
        terms = terms + bgx[i - 1]
    bgf[dp] = terms
    for i in range(1, N_DP):
        push(bgf.at[dp], bgf.at[dp], bg_s.at[2], bg_r.at[2], (off(dp, i, N_DP), ctx))

    third_stage(0)
    last_stage(1)
    last_stage(0)

    arrived(bgf.at[pl.ds(0, 7)], bg_r.at[2])
    terms = bgf[0]
    for p in range(1, N_DP):
        terms = terms + bgf[p]
    bias_out[...] = terms
    last_arrived(1)
    fin_u_out[...] = finu[...]
    last_arrived(0)
    fin_d_out[...] = find[...]

    left_here(kv.at[pl.ds(0, 7)], kv_s.at[0])

    @pl.when(z != 0)
    def _():
        left_here(kv.at[7], kv_s.at[0])

    @pl.when(z == 1)
    def _():
        left_here(kv.at[pl.ds(0, 2)], kv_s.at[0])

    left_here(bb.at[0, pl.ds(0, 7)], bb_s.at[0])
    left_here(bb.at[pl.ds(0, 3)], bb_s.at[1])
    for part in range(2):
        for stage, ref in w_sizes[part].items():
            left_here(ref, w_s.at[part, stage])
        for stage, ref in rs_sizes[part].items():
            left_here(ref, rs_s.at[part, stage])
    left_here(bgz, bg_s.at[0])
    left_here(bgx, bg_s.at[1])
    left_here(bgf.at[pl.ds(0, 7)], bg_s.at[2])

    @pl.when(ctx == 0)
    def _():
        left_here(kv.at[0, :, pl.ds(0, 3 * SINKS), :], sk.at[0])

    @pl.when(z == 0)
    def _():
        left_here(kv.at[0, :, pl.ds(0, 7 * SINKS), :], sk.at[1])


def write_out(fin_u, fin_d, terms, down_out, up_out, bias_out):
    for b in range(4):
        block = jnp.concatenate([fin_u[p, b // 2, 16 * (b % 2) : 16 * (b % 2) + 16, :] for p in range(N_DP)], axis=0)
        up_out[128 * b : 128 * b + 128, :] = block.astype(F32).T
    for e in range(2):
        block = jnp.concatenate([fin_d[4 * e + n // 2, n % 2] for n in range(8)], axis=0)
        down_out[:, e * HEAD_DIM : (e + 1) * HEAD_DIM] = block.astype(F32)
    bias_out[0] = jnp.sum(terms[0:1, :])
    bias_out[1] = jnp.sum(terms[1:2, :])


def on_device(q, k, v, a, h, bias, windows, counts, down, up):
    hbm, smem, vmem = (pl.BlockSpec(memory_space=s) for s in (pl.ANY, pltpu.SMEM, pltpu.VMEM))
    sem = pltpu.SemaphoreType.DMA
    heads = HEADS * HEAD_DIM

    def pair(*dims):
        return [pltpu.VMEM(dims + (rows, HEAD_DIM), BF16) for rows in (UP_ROWS, DOWN_ROWS)]

    scratch = [
        pltpu.VMEM((BLOCKS + 1, KV_HEADS, TOK, 2 * HEAD_DIM), BF16),
        pltpu.VMEM((KV_HEADS, SINKS, 2 * HEAD_DIM), BF16),
        pltpu.VMEM((NX, NZ, 8, HEAD_DIM), F32),
        *pair(2, 2, NX, NY, NZ),
        pltpu.VMEM((TOK, heads), BF16),
        pltpu.VMEM((TOK, a.shape[2]), BF16),
        pltpu.VMEM((TOK, heads), BF16),
        pltpu.VMEM((TOK, heads), BF16),
        pltpu.VMEM((TOK, heads), F32),
        pltpu.VMEM((HEAD_DIM, COLS), BF16),
        pltpu.VMEM((COLS, 2 * HEAD_DIM), BF16),
        pltpu.VMEM((TOK, BLOCKS * TOK), F32),
        pltpu.VMEM((HEAD_STEP, TOK, BLOCKS * TOK), F32),
        pltpu.VMEM((HEAD_STEP, TOK, BLOCKS * TOK), F32),
        *pair(2, 2, NX, NY, NZ),
        *pair(2, NX, NY, NZ),
        *pair(2, 3, 4, NZ),
        *pair(2, 4, NZ),
        *pair(2, 3, NZ),
        *pair(NZ, 2),
        *pair(NZ - 1, 2),
        *pair(N_DP, 2),
        pltpu.VMEM((NZ, NX, 8, HEAD_DIM), F32),
        pltpu.VMEM((NZ - 1, NX, 8, HEAD_DIM), F32),
        pltpu.VMEM((NX, 8, HEAD_DIM), F32),
        pltpu.VMEM((NX - 1, 8, HEAD_DIM), F32),
        pltpu.VMEM((N_DP, 8, HEAD_DIM), F32),
        sem((6,)),
        sem((1,)),
        sem((BLOCKS + 1, KV_HEADS)),
        sem((3,)),
        sem((2,)),
        sem((2,)),
        sem((2, 9)),
        sem((2, 9)),
        sem((2, 8)),
        sem((2, 8)),
        sem((3,)),
        sem((3,)),
    ]
    reduced = pl.pallas_call(
        kernel,
        out_shape=(
            jax.ShapeDtypeStruct((N_DP, 2, UP_ROWS, HEAD_DIM), BF16),
            jax.ShapeDtypeStruct((N_DP, 2, DOWN_ROWS, HEAD_DIM), BF16),
            jax.ShapeDtypeStruct((8, HEAD_DIM), F32),
        ),
        in_specs=[smem] * 3 + [hbm] * 7,
        out_specs=(vmem, vmem, vmem),
        scratch_shapes=scratch,
        compiler_params=pltpu.CompilerParams(
            collective_id=0, has_side_effects=True, vmem_limit_bytes=60 * 1024 * 1024
        ),
        name="token_parallel",
    )(bias, windows, counts, q, k, v, a, h, down, up)
    return pl.pallas_call(
        write_out,
        out_shape=(
            jax.ShapeDtypeStruct(down.shape, F32),
            jax.ShapeDtypeStruct(up.shape, F32),
            jax.ShapeDtypeStruct(bias.shape, F32),
        ),
        in_specs=[vmem] * 3,
        out_specs=(vmem, vmem, smem),
        name="write_out",
    )(*reduced)


def solution(mesh):
    rows = P("dp", "ctx", None)
    placed = (rows,) * 5 + (P("ctx"), P("dp"), P("dp"), P(None, "ctx"), P("ctx", None))
    return jax.shard_map(
        on_device,
        mesh=mesh,
        in_specs=placed,
        out_specs=(P(None, "ctx"), P("ctx", None), P("ctx")),
        check_vma=False,
    )
```

```python
import jax
import jax.numpy as jnp
from jax import lax
from jax.experimental import pallas as pl
from jax.experimental.pallas import tpu as pltpu
from jax.sharding import PartitionSpec as P

NX, NY, NZ = 4, 4, 8
N_CTX, N_DP = NX * NZ, NY * 2
TOK = 128
HEAD_DIM = 128
KV_HEADS = 4
GROUP = 16
HEADS = KV_HEADS * GROUP
RANK = 128
SINKS = 16
BLOCKS = 9
RELAY = 9
UP_ROWS, DOWN_ROWS = 32, 16
HEAD_STEP = 4
MASKED = -1e30
LOG2E = 1.4426950408889634
SCORE_SCALE = LOG2E * HEAD_DIM**-0.5
BF16, F32 = jnp.bfloat16, jnp.float32
MESH = pl.DeviceIdType.MESH

ORDER = (1, 2, 3, 4, 5, 6, 7, 0, 8)
COLS = 10 * TOK


def dot(a, b):
    return lax.dot_general(a, b, (((1,), (0,)), ((), ())), preferred_element_type=F32)


def dot_nt(a, b):
    return lax.dot_general(a, b, (((1,), (1,)), ((), ())), preferred_element_type=F32)


def kernel(
    bias_ref, win_ref, cnt_ref, q_hbm, k_hbm, v_hbm, a_hbm, h_hbm, dw_hbm, uw_hbm,
    fin_u_out, fin_d_out, bias_out,
    kv, sink, bb, wu, wd, q_s, a_s, h_s, o_s, t_s, kt, ve, mask, score_a, score_b,
    gu, gd, rcu, rcd, rau, rad, s2u, s2d, rbu, rbd, s3u, s3d, r3u, r3d, finu, find,
    bg, bgz, bgs, bgx, bgf,
    ld, kv_s, kv_r, sk, bb_s, bb_r, w_s, w_r, rs_s, rs_r, bg_s, bg_r,
):
    dp, ctx = lax.axis_index("dp"), lax.axis_index("ctx")
    y, c, x, z = dp // 2, dp % 2, ctx // NZ, ctx % NZ

    def dev(x_=x, y_=y, z_=z, c_=c):
        return (y_ * 2 + c_, x_ * NZ + z_)

    def off(v, i, n):
        return lax.rem(v + i + n, n)

    right, left = (dp, off(ctx, 1, N_CTX)), (dp, off(ctx, -1, N_CTX))
    jump = (dp, off(ctx, NZ, N_CTX))
    sibling = dev(c_=1 - c)

    def rcopy(src, dst, send, recv, device):
        return pltpu.make_async_remote_copy(
            src_ref=src, dst_ref=dst, send_sem=send, recv_sem=recv, device_id=device, device_id_type=MESH
        )

    def push(src, dst, send, recv, device):
        rcopy(src, dst, send, recv, device).start()

    def arrived(ref, recv):
        rcopy(ref, ref, recv, recv, right).wait_recv()

    def left_here(ref, send):
        rcopy(ref, ref, send, send, right).wait_send()

    for g in range(KV_HEADS):
        cols = pl.ds(g * HEAD_DIM, HEAD_DIM)
        pltpu.make_async_copy(k_hbm.at[0, :, cols], kv.at[0, g, :, pl.ds(0, HEAD_DIM)], ld.at[0]).start()
        pltpu.make_async_copy(v_hbm.at[0, :, cols], kv.at[0, g, :, pl.ds(HEAD_DIM, HEAD_DIM)], ld.at[0]).start()
    for half in range(2):
        rows = pl.multiple_of(dp % 4 * 2 * DOWN_ROWS + half * DOWN_ROWS, DOWN_ROWS)
        cols = pl.multiple_of(dp // 4 * HEAD_DIM, HEAD_DIM)
        pltpu.make_async_copy(
            dw_hbm.at[pl.ds(rows, DOWN_ROWS), pl.ds(cols, HEAD_DIM)], wd.at[half, c, x, y, z], ld.at[1]
        ).start()
        rows = pl.multiple_of(dp * 2 * UP_ROWS + half * UP_ROWS, UP_ROWS)
        pltpu.make_async_copy(uw_hbm.at[pl.ds(rows, UP_ROWS), :], wu.at[half, c, x, y, z], ld.at[2]).start()
    late = [
        pltpu.make_async_copy(q_hbm.at[0], q_s, ld.at[3]),
        pltpu.make_async_copy(a_hbm.at[0], a_s, ld.at[4]),
        pltpu.make_async_copy(h_hbm.at[0], h_s, ld.at[5]),
    ]
    for copy in late:
        copy.start()

    barrier = pltpu.get_barrier_semaphore()
    partners = [left, right]
    partners += [dev(x_=off(x, i, NX)) for i in range(1, NX)]
    partners += [dev(z_=off(z, i, NZ)) for i in range(1, NZ)]
    partners += [(off(dp, i, N_DP), ctx) for i in range(1, N_DP)]
    for partner in partners:
        pl.semaphore_signal(barrier, inc=1, device_id=partner, device_id_type=MESH)
    row8 = lax.broadcasted_iota(jnp.int32, (8, HEAD_DIM), 0)
    bb[x, z] = jnp.where(row8 == 1, bias_ref[1], bias_ref[0]) * LOG2E
    for n, ref in enumerate((kv.at[0], wd.at[:, c, x, y, z], wu.at[:, c, x, y, z])):
        pltpu.make_async_copy(ref, ref, ld.at[n]).wait()

    @pl.when(ctx == 0)
    def _():
        for g in range(KV_HEADS):
            sink[g] = kv[0, g, 0:SINKS, :]

    pl.semaphore_wait(barrier, len(partners))

    first_z = z == 0
    far_slot = jnp.where(first_z, 7, 8)
    far_device = (dp, jnp.where(first_z, x * NZ + NZ - 1, off(ctx, NZ, N_CTX)))

    def kv_push(g, src, dst, device):
        push(kv.at[src, g], kv.at[dst, g], kv_s.at[0], kv_r.at[dst, g], device)

    def kv_arrived(g, slot):
        arrived(kv.at[slot, g], kv_r.at[slot, g])

    def kv_hop(g, step):
        kv_arrived(g, step)
        kv_push(g, step, step + 1, right)
        if step == 1:

            @pl.when(z != 0)
            def _():
                kv_arrived(g, 8)
                kv_push(g, 8, 7, left)

        else:
            kv_arrived(g, 9 - step)
            kv_push(g, 9 - step, 8 - step, left)

    def sink_copies(axis):
        if axis == "x":
            return [rcopy(sink, sink, sk.at[0], sk.at[2], dev(x_=off(x, i, NX))) for i in range(1, NX)]
        return [rcopy(sink, sink, sk.at[1], sk.at[2], dev(z_=off(z, i, NZ))) for i in range(1, NZ)]

    @pl.when(ctx == 0)
    def _():
        for copy in sink_copies("x"):
            copy.start()

    weights = (wd, wu)
    Z_STAGE, SECOND_STAGE, Y_BELOW, Y_ABOVE, Y_ONWARD, X_BELOW, X_ABOVE, X_ONWARD, SIBLING = range(9)
    above, below = off(y, 1, NY), off(y, -1, NY)
    x_above, x_below = off(x, 1, NX), off(x, -1, NX)
    low, high = pl.ds(0, 2), pl.ds(2, 2)

    def w_push(part, stage, src, device):
        push(src, src, w_s.at[part, stage], w_r.at[part, stage], device)

    w_sizes = (
        {
            Z_STAGE: wd.at[0, c, 0, low, pl.ds(0, 7)], SECOND_STAGE: wd.at[0, c, pl.ds(0, 3), low],
            Y_BELOW: wd.at[:, c, 0], Y_ABOVE: wd.at[:, c, 0], Y_ONWARD: wd.at[:, c, 0], SIBLING: wd.at[:, c],
        },
        {
            Z_STAGE: wu.at[0, c, 0, low, pl.ds(0, 7)], SECOND_STAGE: wu.at[0, c, pl.ds(0, 3), low],
            Y_BELOW: wu.at[0, c, 0], Y_ABOVE: wu.at[0, c, 0], Y_ONWARD: wu.at[0, c, 0],
            X_BELOW: wu.at[0, c, 0], X_ABOVE: wu.at[0, c, 0], X_ONWARD: wu.at[0, c, 0], SIBLING: wu.at[:, c],
        },
    )

    def w_arrived(part, stage):
        arrived(w_sizes[part][stage], w_r.at[part, stage])

    def along_z(part):
        for i in range(1, NZ):
            w_push(part, Z_STAGE, weights[part].at[:, c, x, y, z], dev(z_=off(z, i, NZ)))

    def second(part):
        w = weights[part]
        w_arrived(part, Z_STAGE)
        for i in range(1, NX):
            if part == 0:
                w_push(part, SECOND_STAGE, w.at[:, c, x, y], dev(x_=off(x, i, NX)))
            else:
                w_push(part, SECOND_STAGE, w.at[0, c, x, y], dev(x_=off(x, i, NX)))
                w_push(part, SECOND_STAGE, w.at[1, c, x, y], dev(y_=off(y, i, NY)))

    def rings(part):
        w = weights[part]
        w_arrived(part, SECOND_STAGE)
        for half in range(2):
            if part == 1 and half == 1:
                w_push(part, X_BELOW, w.at[1, c, x], dev(x_=x_above))
                w_push(part, X_ABOVE, w.at[1, c, x], dev(x_=x_below))
            else:
                w_push(part, Y_BELOW, w.at[half, c, :, y], dev(y_=above))
                w_push(part, Y_ABOVE, w.at[half, c, :, y], dev(y_=below))

    def y_onward(part):
        w_arrived(part, Y_BELOW)
        from_below = wd.at[0, c, :, below] if part == 0 else wu.at[0, c, low, below]
        w_push(part, Y_ONWARD, from_below, dev(y_=above))
        w_arrived(part, Y_ABOVE)
        from_above = wd.at[1, c, :, above] if part == 0 else wu.at[0, c, high, above]
        w_push(part, Y_ONWARD, from_above, dev(y_=below))

    def x_onward(part):
        w_arrived(part, X_BELOW)
        w_push(part, X_ONWARD, wu.at[1, c, x_below, low], dev(x_=x_above))
        w_arrived(part, X_ABOVE)
        w_push(part, X_ONWARD, wu.at[1, c, x_above, high], dev(x_=x_below))

    def to_sibling(part):
        w_arrived(part, Y_ONWARD)
        if part == 1:
            w_arrived(part, X_ONWARD)
        w_push(part, SIBLING, weights[part].at[:, c], sibling)

    along_z(0)
    for g in range(KV_HEADS):
        kv_push(g, 0, 1, right)
        kv_push(g, 0, far_slot, far_device)
    for i in range(1, NZ):
        push(bb.at[x, z], bb.at[x, z], bb_s.at[0], bb_r.at[0], dev(z_=off(z, i, NZ)))
    along_z(1)

    window, count = win_ref[0], cnt_ref[0]
    row = lax.broadcasted_iota(jnp.int32, (TOK, TOK), 0)
    col = lax.broadcasted_iota(jnp.int32, (TOK, TOK), 1)
    causal = col <= row

    def seen(block):
        return (block * TOK + row - col < window) & ((ctx - block) * TOK + col >= count)

    for j in range(7):
        mask[:, j * TOK : (j + 1) * TOK] = jnp.where(seen(ORDER[j]), 0.0, MASKED)
    both = jnp.where(causal, jnp.where(seen(0), 1, 0), jnp.where(seen(8), 1, 0)) == 1
    mask[:, 7 * TOK : 8 * TOK] = jnp.where(both, 0.0, MASKED)
    sink_seen = (col <= ctx * TOK + row) & (col < count)
    mask[:, 8 * TOK :] = jnp.where(sink_seen, 0.0, MASKED)
    ve[:, HEAD_DIM:] = jnp.ones((COLS, HEAD_DIM), BF16)
    ve[BLOCKS * TOK :, 0:HEAD_DIM] = jnp.zeros((TOK, HEAD_DIM), BF16)
    bg[...] = jnp.zeros(bg.shape, F32)

    second(0)
    for g in range(KV_HEADS):
        kv_hop(g, 1)

    @pl.when(z == 1)
    def _():
        for g in range(KV_HEADS):
            kv_push(g, 1, RELAY, jump)


    @pl.when((z == 0) & (x != 0))
    def _():
        arrived(sink, sk.at[2])

    @pl.when(z == 0)
    def _():
        for copy in sink_copies("z"):
            copy.start()

    arrived(bb.at[0, pl.ds(0, 7)], bb_r.at[0])
    for i in range(1, NX):
        push(bb.at[x], bb.at[x], bb_s.at[1], bb_r.at[1], dev(x_=off(x, i, NX)))
    second(1)
    rings(0)

    for g in range(KV_HEADS):
        kv_hop(g, 2)


    arrived(bb.at[pl.ds(0, 3)], bb_r.at[1])

    @pl.when(z != 0)
    def _():
        arrived(sink, sk.at[2])

    for g in range(KV_HEADS):
        kv_hop(g, 3)

    @pl.when(z == 1)
    def _():
        for g in range(KV_HEADS):
            kv_arrived(g, RELAY)
            kv_push(g, RELAY, 8, left)

    rings(1)
    y_onward(0)
    late[0].wait()

    def columns(head):
        return pl.ds(pl.multiple_of(head * HEAD_DIM, HEAD_DIM), HEAD_DIM)

    rows = HEAD_STEP * TOK

    def score_heads(first, score_s):
        queries = jnp.concatenate([q_s[:, columns(first + e)] for e in range(HEAD_STEP)], axis=0)
        score = (dot(queries, kt[...]) * SCORE_SCALE).reshape(HEAD_STEP, TOK, COLS)

        def tile(j):
            return score[:, :, j * TOK : (j + 1) * TOK]

        biases = []
        for e in range(HEAD_STEP):
            shard = (first + e) // 2
            biases.append(bb[shard // NZ, shard % NZ, e % 2 : e % 2 + 1, :][None])
        top = None
        for j in range(BLOCKS):
            seen_j = mask[:, j * TOK : (j + 1) * TOK][None]
            if j < 7:
                part = tile(j) + seen_j
            elif j == 7:
                part = jnp.where(causal[None], tile(7), tile(8)) + seen_j
            else:
                part = tile(9) + (seen_j + jnp.concatenate(biases, axis=0))
            score_s[:, :, j * TOK : (j + 1) * TOK] = part
            top = part if top is None else jnp.maximum(top, part)
        return jnp.max(top, axis=-1, keepdims=True)

    def finish_heads(first, score_s, top):
        probs = [jnp.exp2(score_s[:, :, j * TOK : (j + 1) * TOK] - top).astype(BF16) for j in range(BLOCKS)]
        nothing = jnp.zeros((), BF16)
        near = jnp.where(causal[None], probs[7], nothing)
        far = jnp.where(causal[None], nothing, probs[7])
        local = jnp.concatenate(probs[:7] + [near, far], axis=-1).reshape(rows, BLOCKS * TOK)
        from_sinks = dot(probs[8].reshape(rows, TOK), ve[BLOCKS * TOK :, :])
        total = dot(local, ve[0 : BLOCKS * TOK, :]) + from_sinks
        scale = 1.0 / total[:, HEAD_DIM:]
        out = (total[:, 0:HEAD_DIM] * scale).astype(BF16)
        term = (from_sinks[:, 0:HEAD_DIM] - from_sinks[:, HEAD_DIM:] * out.astype(F32)) * scale
        for e in range(HEAD_STEP):
            o_s[:, columns(first + e)] = out[e * TOK : (e + 1) * TOK]
            t_s[:, columns(first + e)] = term[e * TOK : (e + 1) * TOK]

    def attend_heads(first):
        steps = GROUP // HEAD_STEP
        held = (score_a, score_b)
        top = score_heads(first, held[0])
        for n in range(steps):
            later = score_heads(first + (n + 1) * HEAD_STEP, held[(n + 1) % 2]) if n + 1 < steps else None
            finish_heads(first + n * HEAD_STEP, held[n % 2], top)
            top = later

    def attend_group(g, carry):
        kv_arrived(g, 4)
        kv_arrived(g, 5)

        @pl.when(first_z)
        def _():
            kv_arrived(g, 8)

        for j, block in enumerate(ORDER):
            kt[:, j * TOK : (j + 1) * TOK] = kv[block, g, :, 0:HEAD_DIM].T
            ve[j * TOK : (j + 1) * TOK, 0:HEAD_DIM] = kv[block, g, :, HEAD_DIM:]
        padded = jnp.concatenate([sink[g, :, 0:HEAD_DIM], jnp.zeros((TOK - SINKS, HEAD_DIM), BF16)], axis=0)
        kt[:, BLOCKS * TOK :] = padded.T
        ve[BLOCKS * TOK : BLOCKS * TOK + SINKS, 0:HEAD_DIM] = sink[g, :, HEAD_DIM:]
        attend_heads(g * GROUP)

        @pl.when(g == 0)
        def _():
            y_onward(1)
            x_onward(1)

        @pl.when(g == 1)
        def _():
            to_sibling(0)

        @pl.when(g == 2)
        def _():
            to_sibling(1)

        return carry

    lax.fori_loop(0, KV_HEADS, attend_group, 0)

    pieces = [(half, p % 2, p // 2) for p in range(N_DP) for half in range(2)]

    def down_weight(xs, zs):
        return [
            jnp.concatenate([wd[half, cs, xs, ys, zs] for half, cs, ys in pieces[8 * e : 8 * e + 8]], axis=0)
            for e in range(2)
        ]

    w_arrived(0, SIBLING)

    def low_out_step(xs, total):
        down = jnp.concatenate([w for zs in range(NZ) for w in down_weight(xs, zs)], axis=1)
        return total + dot_nt(down, o_s[:, pl.ds(pl.multiple_of(xs * 2048, 2048), 2048)])

    low_out_t = lax.fori_loop(0, NX, low_out_step, jnp.zeros((RANK, TOK), F32)).astype(BF16)
    late[1].wait()

    grads, from_core = (gd, gu), (rcd, rcu)
    first_in, first_sum = (rad, rau), (s2d, s2u)
    second_in, second_sum = (rbd, rbu), (s3d, s3u)
    third_in, final = (r3d, r3u), (find, finu)
    order = [off(x, i, NX) for i in (1, 2, 3, 0)]

    CORE, FIRST, SECOND, THIRD, LAST = 0, 4, 5, 6, 7
    rs_sizes = [
        {CORE: from_core[p], FIRST: first_in[p], SECOND: second_in[p], THIRD: third_in[p], LAST: final[p].at[pl.ds(0, 7)]}
        for p in range(2)
    ]

    def rs_push(part, stage, src, dst, device, row=0):
        push(src, dst, rs_s.at[part, stage], rs_r.at[part, stage + row], device)

    def rs_arrived(part, stage):
        arrived(rs_sizes[part][stage], rs_r.at[part, stage])

    def to_core(part, j):
        xs = order[j]
        rs_push(part, CORE, grads[part].at[:, 1 - c, xs], from_core[part].at[:, xs], sibling, j)

    def first_stage(part, j):
        xs = order[j]
        arrived(from_core[part].at[:, xs], rs_r.at[part, j])
        mine, theirs = grads[part], from_core[part]

        def one(n, carry):
            half, ys = n // NY, n % NY
            mine[half, c, xs, ys] = (mine[half, c, xs, ys].astype(F32) + theirs[half, xs, ys].astype(F32)).astype(BF16)
            return carry

        lax.fori_loop(0, 2 * NY, one, 0)
        for i in range(1, NY):
            rs_push(part, FIRST, mine.at[0, c, xs, off(y, i, NY)], first_in[part].at[0, i - 1, xs], dev(y_=off(y, i, NY)))
        if j < 3:
            rs_push(part, FIRST, mine.at[1, c, xs], first_in[part].at[1, j], dev(x_=xs))

    def second_stage(part):
        rs_arrived(part, FIRST)
        mine, theirs, total = grads[part], first_in[part], first_sum[part]

        def one(n, carry):
            for half, own in ((0, mine.at[0, c, n, y]), (1, mine.at[1, c, x, n])):
                acc = own[...].astype(F32)
                for i in range(3):
                    acc = acc + theirs[half, i, n].astype(F32)
                total[half, n] = acc.astype(BF16)
            return carry

        lax.fori_loop(0, 4, one, 0)
        for i in range(1, NX):
            to_x, to_y = off(x, i, NX), off(y, i, NY)
            rs_push(part, SECOND, total.at[0, to_x], second_in[part].at[0, i - 1], dev(x_=to_x))
            rs_push(part, SECOND, total.at[1, to_y], second_in[part].at[1, i - 1], dev(y_=to_y))

    def third_stage(part):
        rs_arrived(part, SECOND)
        mine, theirs, total = first_sum[part], second_in[part], second_sum[part]
        for half, own in ((0, x), (1, y)):
            acc = mine[half, own].astype(F32)
            for i in range(3):
                acc = acc + theirs[half, i].astype(F32)
            total[:, half] = acc.astype(BF16)
        for i in range(1, NZ):
            rs_push(part, THIRD, total.at[off(z, i, NZ)], third_in[part].at[i - 1], dev(z_=off(z, i, NZ)))

    def last_stage(part):
        rs_arrived(part, THIRD)
        acc = second_sum[part][z].astype(F32)
        for i in range(1, NZ):
            acc = acc + third_in[part][i - 1].astype(F32)
        final[part][dp] = acc.astype(BF16)
        for i in range(1, N_DP):
            rs_push(part, LAST, final[part].at[dp], final[part].at[dp], (off(dp, i, N_DP), ctx))

    def last_arrived(part):
        rs_arrived(part, LAST)

    def up_row(xs):
        def step(zs, carry):
            cols = pl.ds(pl.multiple_of((xs * NZ + zs) * 512, 512), 512)
            grad = (2.0 * dot(low_out_t, a_s[:, cols])).astype(BF16)
            for p in range(N_DP):
                for half in range(2):
                    for j in range(2):
                        lane = 256 * half + 128 * j
                        gu[half, p % 2, xs, p // 2, zs, 16 * j : 16 * j + 16, :] = grad[
                            16 * p : 16 * p + 16, lane : lane + 128
                        ]
            return carry

        lax.fori_loop(0, NZ, step, 0, unroll=4)

    for j in range(NX):
        up_row(order[j])
        to_core(1, j)
        if j > 0:
            first_stage(1, j - 1)
    first_stage(1, 3)

    w_arrived(1, SIBLING)

    def low_grad_step(xs, total):
        up = jnp.concatenate(
            [wu[half, cs, xs, ys, zs] for zs in range(NZ) for half, cs, ys in pieces], axis=0
        )
        return total + dot(a_s[:, pl.ds(pl.multiple_of(xs * 4096, 4096), 4096)], up)

    low_grad = lax.fori_loop(0, NX, low_grad_step, jnp.zeros((TOK, RANK), F32))
    low_grad_t = low_grad.T.astype(BF16)
    low_grad = low_grad.astype(BF16)
    late[2].wait()

    def down_row(xs):
        def step(zs, carry):
            cols = pl.ds(pl.multiple_of((xs * NZ + zs) * 256, 256), 256)
            down = jnp.concatenate(down_weight(xs, zs), axis=1)
            head_total = (h_s[:, cols].astype(F32) + 2.0 * dot(low_grad, down)).astype(BF16)
            bias_terms = jnp.sum(head_total.astype(F32) * t_s[:, cols], axis=0, keepdims=True)
            for e in range(2):
                bg[zs, xs, e : e + 1, :] = bias_terms[:, e * HEAD_DIM : (e + 1) * HEAD_DIM]
            grad = (2.0 * dot(low_grad_t, o_s[:, cols])).astype(BF16)
            for n, (half, cs, ys) in enumerate(pieces):
                e, r = n // 8, n % 8 * DOWN_ROWS
                gd[half, cs, xs, ys, zs] = grad[r : r + DOWN_ROWS, e * HEAD_DIM : (e + 1) * HEAD_DIM]
            return carry

        lax.fori_loop(0, NZ, step, 0, unroll=4)

    for j in range(NX):
        down_row(order[j])
        to_core(0, j)
        if j > 0:
            first_stage(0, j - 1)

    for i in range(1, NZ):
        push(bg.at[off(z, i, NZ)], bgz.at[i - 1], bg_s.at[0], bg_r.at[0], dev(z_=off(z, i, NZ)))
    first_stage(0, 3)
    second_stage(1)

    arrived(bgz, bg_r.at[0])
    terms = bg[z]
    for i in range(1, NZ):
        terms = terms + bgz[i - 1]
    bgs[...] = terms
    for i in range(1, NX):
        push(bgs.at[off(x, i, NX)], bgx.at[i - 1], bg_s.at[1], bg_r.at[1], dev(x_=off(x, i, NX)))

    second_stage(0)
    third_stage(1)

    arrived(bgx, bg_r.at[1])
    terms = bgs[x]
    for i in range(1, NX):
        terms = terms + bgx[i - 1]
    bgf[dp] = terms
    for i in range(1, N_DP):
        push(bgf.at[dp], bgf.at[dp], bg_s.at[2], bg_r.at[2], (off(dp, i, N_DP), ctx))

    third_stage(0)

    left_here(kv.at[pl.ds(0, 7)], kv_s.at[0])

    @pl.when(z != 0)
    def _():
        left_here(kv.at[7], kv_s.at[0])

    @pl.when(z == 1)
    def _():
        left_here(kv.at[pl.ds(0, 2)], kv_s.at[0])

    left_here(bb.at[0, pl.ds(0, 7)], bb_s.at[0])
    left_here(bb.at[pl.ds(0, 3)], bb_s.at[1])
    for part in range(2):
        for stage, ref in w_sizes[part].items():
            left_here(ref, w_s.at[part, stage])
        for stage in (CORE, FIRST):
            left_here(rs_sizes[part][stage], rs_s.at[part, stage])

    @pl.when(ctx == 0)
    def _():
        left_here(kv.at[0, :, pl.ds(0, 3 * SINKS), :], sk.at[0])

    @pl.when(z == 0)
    def _():
        left_here(kv.at[0, :, pl.ds(0, 7 * SINKS), :], sk.at[1])

    last_stage(1)
    last_stage(0)

    arrived(bgf.at[pl.ds(0, 7)], bg_r.at[2])
    terms = bgf[0]
    for p in range(1, N_DP):
        terms = terms + bgf[p]
    bias_out[...] = terms
    last_arrived(1)
    fin_u_out[...] = finu[...]
    last_arrived(0)
    fin_d_out[...] = find[...]

    for part in range(2):
        for stage in (SECOND, THIRD, LAST):
            left_here(rs_sizes[part][stage], rs_s.at[part, stage])
    left_here(bgz, bg_s.at[0])
    left_here(bgx, bg_s.at[1])
    left_here(bgf.at[pl.ds(0, 7)], bg_s.at[2])


def write_out(fin_u, fin_d, terms, down_out, up_out, bias_out):
    for b in range(4):
        block = jnp.concatenate([fin_u[p, b // 2, 16 * (b % 2) : 16 * (b % 2) + 16, :] for p in range(N_DP)], axis=0)
        up_out[128 * b : 128 * b + 128, :] = block.astype(F32).T
    for e in range(2):
        block = jnp.concatenate([fin_d[4 * e + n // 2, n % 2] for n in range(8)], axis=0)
        down_out[:, e * HEAD_DIM : (e + 1) * HEAD_DIM] = block.astype(F32)
    bias_out[0] = jnp.sum(terms[0:1, :])
    bias_out[1] = jnp.sum(terms[1:2, :])


def on_device(q, k, v, a, h, bias, windows, counts, down, up):
    hbm, smem, vmem = (pl.BlockSpec(memory_space=s) for s in (pl.ANY, pltpu.SMEM, pltpu.VMEM))
    sem = pltpu.SemaphoreType.DMA
    heads = HEADS * HEAD_DIM

    def pair(*dims):
        return [pltpu.VMEM(dims + (rows, HEAD_DIM), BF16) for rows in (UP_ROWS, DOWN_ROWS)]

    scratch = [
        pltpu.VMEM((BLOCKS + 1, KV_HEADS, TOK, 2 * HEAD_DIM), BF16),
        pltpu.VMEM((KV_HEADS, SINKS, 2 * HEAD_DIM), BF16),
        pltpu.VMEM((NX, NZ, 8, HEAD_DIM), F32),
        *pair(2, 2, NX, NY, NZ),
        pltpu.VMEM((TOK, heads), BF16),
        pltpu.VMEM((TOK, a.shape[2]), BF16),
        pltpu.VMEM((TOK, heads), BF16),
        pltpu.VMEM((TOK, heads), BF16),
        pltpu.VMEM((TOK, heads), F32),
        pltpu.VMEM((HEAD_DIM, COLS), BF16),
        pltpu.VMEM((COLS, 2 * HEAD_DIM), BF16),
        pltpu.VMEM((TOK, BLOCKS * TOK), F32),
        pltpu.VMEM((HEAD_STEP, TOK, BLOCKS * TOK), F32),
        pltpu.VMEM((HEAD_STEP, TOK, BLOCKS * TOK), F32),
        *pair(2, 2, NX, NY, NZ),
        *pair(2, NX, NY, NZ),
        *pair(2, 3, 4, NZ),
        *pair(2, 4, NZ),
        *pair(2, 3, NZ),
        *pair(NZ, 2),
        *pair(NZ - 1, 2),
        *pair(N_DP, 2),
        pltpu.VMEM((NZ, NX, 8, HEAD_DIM), F32),
        pltpu.VMEM((NZ - 1, NX, 8, HEAD_DIM), F32),
        pltpu.VMEM((NX, 8, HEAD_DIM), F32),
        pltpu.VMEM((NX - 1, 8, HEAD_DIM), F32),
        pltpu.VMEM((N_DP, 8, HEAD_DIM), F32),
        sem((6,)),
        sem((1,)),
        sem((BLOCKS + 1, KV_HEADS)),
        sem((3,)),
        sem((2,)),
        sem((2,)),
        sem((2, 9)),
        sem((2, 9)),
        sem((2, 8)),
        sem((2, 8)),
        sem((3,)),
        sem((3,)),
    ]
    reduced = pl.pallas_call(
        kernel,
        out_shape=(
            jax.ShapeDtypeStruct((N_DP, 2, UP_ROWS, HEAD_DIM), BF16),
            jax.ShapeDtypeStruct((N_DP, 2, DOWN_ROWS, HEAD_DIM), BF16),
            jax.ShapeDtypeStruct((8, HEAD_DIM), F32),
        ),
        in_specs=[smem] * 3 + [hbm] * 7,
        out_specs=(vmem, vmem, vmem),
        scratch_shapes=scratch,
        compiler_params=pltpu.CompilerParams(
            collective_id=0, has_side_effects=True, vmem_limit_bytes=60 * 1024 * 1024
        ),
        name="token_parallel",
    )(bias, windows, counts, q, k, v, a, h, down, up)
    return pl.pallas_call(
        write_out,
        out_shape=(
            jax.ShapeDtypeStruct(down.shape, F32),
            jax.ShapeDtypeStruct(up.shape, F32),
            jax.ShapeDtypeStruct(bias.shape, F32),
        ),
        in_specs=[vmem] * 3,
        out_specs=(vmem, vmem, smem),
        name="write_out",
    )(*reduced)


def solution(mesh):
    rows = P("dp", "ctx", None)
    placed = (rows,) * 5 + (P("ctx"), P("dp"), P("dp"), P(None, "ctx"), P("ctx", None))
    return jax.shard_map(
        on_device,
        mesh=mesh,
        in_specs=placed,
        out_specs=(P(None, "ctx"), P("ctx", None), P("ctx")),
        check_vma=False,
    )
```
